256 devices in a mesh: frames: 64 (over z, y, core), heads: 4 (over x).
Axes of the slice: x: 4, y: 4, z: 8, core: 2. Of those that a mesh axis runs over, the one named last changes fastest.
Arguments:
- query_in: bfloat16 [8192, 5120], P(('frames', 'heads')), may hold values from -6 to 6
- key_in: bfloat16 [8192, 5120], P(('frames', 'heads')), may hold values from -6 to 6
- value_in: bfloat16 [8192, 5120], P(('frames', 'heads')), may hold values from -6 to 6
- query_gain: float32 [5120], replicated, may hold values from 1.2 to 8
- key_gain: float32 [5120], replicated, may hold values from 1.2 to 8
- keep_flags: int32 [64, 64], P('frames'), may hold values from 0 to 1, as said below
- pool_levels: int32 [64, 64], P('frames'), may hold values from 0 to 3, as said below
- live_counts: int32 [64], replicated, may hold values from 64 to 128, as said below
Outputs:
- attended: bfloat16 [8192, 5120], P(('frames', 'heads'))
The draws below stay inside these ranges and needn't reach their ends.
Inputs may be any that keep to these rules, and one draw needn't show every extreme that they name: keep_flags[i, i] = 1; for j - i = +-2^k with k < 3 an entry is 0 or 1; all others are 0. For j - i = +-2^k with k < 3, pool_levels[i, j] is k or k + 1; all others are 0. `live_counts`: some frame has all of its tokens live.
All inputs are finite; a program needn't handle non-finite values.
Results may differ from the reference program's by a relative error of at most 0.01.
The reference program's roundings to bfloat16 on the way (of `query_rot`, `key_rot` and `shares`) count: a program that leaves them out, or rounds other values in their place, can miss the bound.
Values may be sent and summed in bfloat16 or wider, within the bound.
No kernel may reach another device: no remote copies, remote signals or barrier semaphores. Data moves between devices by JAX's collectives and lax.ppermute only.
A program may use at most 128 MiB of HBM per device.

```python
import math
import jax
import jax.numpy as jnp
from jax import lax

HEADS = 40
HDIM = 128
D = 5120
PH = 4
PW = 32
LEVELS = 3
FRAMES = 64
TOKENS = 8192


def draw_query_in(key, part):
    key = jax.random.fold_in(key, 21)
    own_key = jax.random.fold_in(key, 0)
    result = jax.random.normal(own_key, (TOKENS, D), jnp.float32)
    return jnp.clip(result, -6.0, 6.0).astype(jnp.bfloat16)


def draw_key_in(key, part):
    key = jax.random.fold_in(key, 22)
    result = jax.random.normal(key, (TOKENS, D), jnp.float32)
    return jnp.clip(result, -6.0, 6.0).astype(jnp.bfloat16)


def spread_gain(key, low_end, high_end):
    return jnp.exp(jax.random.uniform(key, (D,), jnp.float32, jnp.log(low_end), jnp.log(high_end)))


def draw_query_gain(key, part):
    key = jax.random.fold_in(key, 31)
    return spread_gain(key, 1.2, 2.4)


def draw_key_gain(key, part):
    key = jax.random.fold_in(key, 32)
    return spread_gain(key, 1.2, 2.4)


def distance_table():
    rows_index = jnp.arange(FRAMES, dtype=jnp.int32)[:, None]
    cols_index = jnp.arange(FRAMES, dtype=jnp.int32)[None, :]
    frame_gap = jnp.abs(cols_index - rows_index)
    allowed = jnp.zeros((FRAMES, FRAMES), bool)
    base_level = jnp.zeros((FRAMES, FRAMES), jnp.int32)
    for level_index in range(LEVELS):
        hit = frame_gap == 2 ** level_index
        allowed = allowed | hit
        base_level = jnp.where(hit, level_index, base_level)
    return (frame_gap, allowed, base_level)


def draw_keep_flags(key, part):
    key = jax.random.fold_in(key, 11)
    frame_gap, allowed, base_level = distance_table()
    coin = jax.random.randint(key, (FRAMES, FRAMES), 0, 4)
    kept = jnp.where(frame_gap == 0, 1, jnp.where(allowed & (coin > 0), 1, 0))
    return kept.astype(jnp.int32)


def draw_pool_levels(key, part):
    key = jax.random.fold_in(key, 12)
    frame_gap, allowed, base_level = distance_table()
    extra = jax.random.randint(key, (FRAMES, FRAMES), 0, 2)
    return jnp.where(allowed, base_level + extra, 0).astype(jnp.int32)


def draw_live_counts(key, part):
    key = jax.random.fold_in(key, 13)
    count_key, full_key = jax.random.split(key)
    frame_tokens = PH * PW
    drawn = jax.random.randint(count_key, (FRAMES,), frame_tokens // 2, frame_tokens + 1)
    full_frame = jax.random.randint(full_key, (), 0, FRAMES)
    return jnp.where(jnp.arange(FRAMES, dtype=jnp.int32) == full_frame, frame_tokens, drawn).astype(jnp.int32)


def block_levels(stream_key, extent, cuts, smallest, top_value):
    loudness, own = 1.0, jax.random.fold_in(stream_key, 6)
    for axis_at, shards_of in cuts:
        heights = jnp.exp(jax.random.uniform(jax.random.fold_in(own, axis_at), (shards_of,), jnp.float32, smallest / len(cuts), top_value / len(cuts)))
        loudness = loudness * jnp.repeat(heights, extent[axis_at] // shards_of).reshape([-1 if axis == axis_at else 1 for axis in range(len(extent))])
    return loudness


def bell_draw(key, dims, spread, limit, cuts=(), kind=jnp.bfloat16):
    values = jax.random.normal(key, dims, jnp.float32) * spread
    if len(cuts) > 0:
        values = block_levels(key, dims, cuts, -0.22, 0.18) * values
    return jnp.clip(values, min=-limit, max=limit).astype(kind)


def setup_inputs(seed: int = 0) -> dict:
    keys = jax.random.split(jax.random.key(seed), 9)
    return {
        "query_in": draw_query_in(jax.random.fold_in(keys[8], 71), 0),
        "key_in": draw_key_in(jax.random.fold_in(keys[8], 71), 0),
        "value_in": bell_draw(keys[2], (TOKENS, D), 1.0, 6.0, ((0, 256),)),
        "query_gain": draw_query_gain(jax.random.fold_in(keys[8], 71), 0),
        "key_gain": draw_key_gain(jax.random.fold_in(keys[8], 71), 0),
        "keep_flags": draw_keep_flags(jax.random.fold_in(keys[8], 71), 0),
        "pool_levels": draw_pool_levels(jax.random.fold_in(keys[8], 71), 0),
        "live_counts": draw_live_counts(jax.random.fold_in(keys[8], 71), 0),
    }


epsilon = 1e-06
floor_score = -1e+30

def rope_angles(frame_pos, row_pos, col_pos, half_pairs):
    space_pairs = half_pairs // 3
    time_pairs = half_pairs - 2 * space_pairs

    def freq_table(pair_count):
        return 1.0 / 10000.0 ** (jnp.arange(pair_count).astype(jnp.float32) / pair_count)
    return jnp.concatenate([frame_pos[:, None] * freq_table(time_pairs)[None, :], row_pos[:, None] * freq_table(space_pairs)[None, :], col_pos[:, None] * freq_table(space_pairs)[None, :]], axis=1)

def normalize_rope(inputs, gain, angles):
    row_count = inputs.shape[0]
    head_count = inputs.shape[1] // HDIM
    floats = inputs.astype(jnp.float32)
    scaled = floats * lax.rsqrt(lax.optimization_barrier(jnp.mean(floats * floats, axis=1, keepdims=True)) + epsilon) * gain[None, :]
    paired = scaled.reshape(row_count, head_count, HDIM // 2, 2)
    cosine_table = jnp.cos(angles)[:, None, :]
    sine_table = jnp.sin(angles)[:, None, :]
    real_part = paired[..., 0]
    imag_part = paired[..., 1]
    turned = jnp.stack([real_part * cosine_table - imag_part * sine_table, real_part * sine_table + imag_part * cosine_table], axis=-1)
    return turned.reshape(row_count, head_count * HDIM).astype(jnp.bfloat16)

def group_counts(live_total, frame_tokens, level):
    group_width = 2 ** level
    starts = jnp.arange(frame_tokens // group_width, dtype=jnp.int32) * group_width
    return jnp.clip(live_total - starts, 0, group_width).astype(jnp.int32)

def pool_pair(values, weights):
    half_rows = values.shape[0] // 2
    paired = values.reshape(half_rows, 2, values.shape[1]).astype(jnp.float32)
    amount = weights.reshape(half_rows, 2).astype(jnp.float32)
    summed = paired[:, 0] * amount[:, 0:1] + paired[:, 1] * amount[:, 1:2]
    return (summed / jnp.maximum(amount[:, 0] + amount[:, 1], 1.0)[:, None]).astype(jnp.bfloat16)

def fresh_state(head_count, frame_tokens):
    return (jnp.full((head_count, frame_tokens), floor_score, jnp.float32), jnp.zeros((head_count, frame_tokens), jnp.float32), jnp.zeros((head_count, frame_tokens, HDIM), jnp.float32))

def absorb(carry_state, query_heads, key_rows, value_rows, group_weights, active_flag):
    key_count = key_rows.shape[0]
    head_count = query_heads.shape[1]
    key_heads = key_rows.reshape(key_count, head_count, HDIM).astype(jnp.float32)
    value_heads = value_rows.reshape(key_count, head_count, HDIM).astype(jnp.float32)
    scores = jnp.einsum('qhd,khd->hqk', query_heads.astype(jnp.float32), key_heads) / math.sqrt(HDIM)
    score_bias = jnp.where(group_weights > 0, jnp.log(jnp.maximum(group_weights, 1).astype(jnp.float32)), floor_score)
    scores = jnp.where(active_flag, scores + score_bias[None, None, :], floor_score)
    running_max, running_sum, numerator = carry_state
    new_max = jnp.maximum(running_max, lax.optimization_barrier(jnp.max(scores, axis=2)))
    probs = jnp.exp(scores - new_max[:, :, None])
    factor = jnp.exp(running_max - new_max)
    running_sum = running_sum * factor + lax.optimization_barrier(jnp.sum(probs, axis=2))
    shares = probs.astype(jnp.bfloat16)
    numerator = numerator * factor[:, :, None] + jnp.einsum('hqk,khd->hqd', shares.astype(jnp.float32), value_heads)
    return (new_max, running_sum, numerator)

def finish(carry_state, live_total, frame_tokens):
    running_max, running_sum, numerator = carry_state
    result = numerator / running_sum[:, :, None]
    head_count = result.shape[0]
    ordered = jnp.transpose(result, (1, 0, 2)).reshape(frame_tokens, head_count * HDIM)
    alive = (jnp.arange(frame_tokens, dtype=jnp.int32) < live_total)[:, None]
    return jnp.where(alive, ordered, 0.0).astype(jnp.bfloat16)

def tile_plan():
    plan = [(0, 0)]
    for level_index in range(LEVELS):
        for direction in (1, -1):
            for level in (level_index, level_index + 1):
                plan.append((direction * 2 ** level_index, level))
    return plan

def reference(query_in, key_in, value_in, query_gain, key_gain, keep_flags, pool_levels, live_counts):
    frame_tokens = PH * PW
    token_index = jnp.arange(TOKENS, dtype=jnp.int32)
    inner_index = token_index % frame_tokens
    angles = rope_angles((token_index // frame_tokens).astype(jnp.float32), (inner_index // PW).astype(jnp.float32), (inner_index % PW).astype(jnp.float32), HDIM // 2)
    query_rot = normalize_rope(query_in, query_gain, angles).reshape(FRAMES, frame_tokens, D)
    key_rot = normalize_rope(key_in, key_gain, angles).reshape(FRAMES, frame_tokens, D)
    value_frames = value_in.reshape(FRAMES, frame_tokens, D)
    key_levels = [key_rot]
    value_levels = [value_frames]
    for level in range(LEVELS):
        weights = jax.vmap(lambda frame_total: group_counts(frame_total, frame_tokens, level))(live_counts)
        key_levels.append(jax.vmap(pool_pair)(key_levels[-1], weights))
        value_levels.append(jax.vmap(pool_pair)(value_levels[-1], weights))

    def one_frame(frame_index):
        query_heads = query_rot[frame_index].reshape(frame_tokens, HEADS, HDIM)
        carry_state = fresh_state(HEADS, frame_tokens)
        for distance, level in tile_plan():
            source_frame = frame_index + distance
            inside = (source_frame >= 0) & (source_frame < FRAMES)
            source_clipped = jnp.clip(source_frame, 0, FRAMES - 1).astype(jnp.int32)
            active_flag = inside & (keep_flags[frame_index, source_clipped] == 1) & (pool_levels[frame_index, source_clipped] == level)
            group_weights = group_counts(live_counts[source_clipped], frame_tokens, level)
            carry_state = absorb(carry_state, query_heads, key_levels[level][source_clipped], value_levels[level][source_clipped], group_weights, active_flag)
        return finish(carry_state, live_counts[frame_index], frame_tokens)
    result = lax.map(one_frame, jnp.arange(FRAMES, dtype=jnp.int32))
    return result.reshape(TOKENS, D)
```

```python
import math

import jax
import jax.numpy as jnp
import numpy as np
from jax import lax
from jax.experimental import pallas as pl
from jax.experimental.pallas import tpu as pltpu
from jax.sharding import PartitionSpec as P

HDIM = 128
PW = 32
LEVELS = 3
EPSILON = 1e-06
FLOOR = -1e30
LOG2E = math.log2(math.e)


def frequency_rows():
    half = HDIM // 2
    third = half // 3
    lead = half - 2 * third
    rows = np.zeros((8, HDIM), np.float64)
    for lane in range(HDIM):
        i = lane // 2
        if i < lead:
            rows[0, lane] = 10000.0 ** (-i / lead)
        elif i < lead + third:
            rows[1, lane] = 10000.0 ** (-(i - lead) / third)
        else:
            rows[2, lane] = 10000.0 ** (-(i - lead - third) / third)
    return rows.astype(np.float32)


def prepare_kernel(q_ref, k_ref, v_ref, qg_ref, kg_ref, freq_ref, kv_ref, qo_ref):
    rows, width = q_ref.shape
    parts, _, part_width = qo_ref.shape
    frame = lax.axis_index("frames")
    first = lax.axis_index("heads") * rows
    token = first + lax.broadcasted_iota(jnp.int32, (rows, HDIM), 0)
    lane = lax.broadcasted_iota(jnp.int32, (rows, HDIM), 1)
    even = lane % 2 == 0
    freq = freq_ref[...]
    angles = (
        frame.astype(jnp.float32) * freq[0:1]
        + (token // PW).astype(jnp.float32) * freq[1:2]
        + (token % PW).astype(jnp.float32) * freq[2:3]
    )
    cosine = jnp.cos(angles)
    sine = jnp.where(even, -jnp.sin(angles), jnp.sin(angles))

    def turn(x_ref, gain_ref, out_ref):
        floats = x_ref[...].astype(jnp.float32)
        inverse = lax.rsqrt(jnp.mean(floats * floats, axis=1, keepdims=True) + EPSILON)
        gain = gain_ref[...]
        for head in range(width // HDIM):
            at = head * HDIM
            scaled = floats[:, at : at + HDIM] * inverse * gain[:, at : at + HDIM]
            partner = jnp.where(
                even, pltpu.roll(scaled, HDIM - 1, 1), pltpu.roll(scaled, 1, 1)
            )
            turned = (scaled * cosine + partner * sine).astype(jnp.bfloat16)
            part, offset = at // part_width, at % part_width
            out_ref[part, :, offset : offset + HDIM] = turned

    turn(k_ref, kg_ref, kv_ref)
    for part in range(parts):
        kv_ref[part, :, part_width:] = v_ref[:, part * part_width : (part + 1) * part_width]
    turn(q_ref, qg_ref, qo_ref)


def weights_of(live, index, group):
    return jnp.clip(live - index * group, 0, group)


def pooled(values, live, level):
    count = values.shape[0]
    half = count // 2
    group = 2**level
    out_row = lax.broadcasted_iota(jnp.int32, (half, count), 0)
    in_row = lax.broadcasted_iota(jnp.int32, (half, count), 1)
    mix = jnp.where(in_row // 2 == out_row, weights_of(live, in_row, group), 0)
    total = weights_of(live, lax.broadcasted_iota(jnp.int32, (half, 1), 0), 2 * group)
    summed = jnp.dot(
        mix.astype(jnp.float32).astype(jnp.bfloat16), values, preferred_element_type=jnp.float32
    )
    return (summed / jnp.maximum(total, 1).astype(jnp.float32)).astype(jnp.bfloat16)


def pool_kernel(live_ref, kv_ref, one_ref, two_ref):
    live = live_ref[lax.axis_index("frames")]
    one = pooled(kv_ref[...], live, 0)
    one_ref[...] = one
    two_ref[...] = pooled(one, live, 1)


def selected(values, live, level, chosen):
    count = values.shape[0]
    group = 2**level
    out_row = lax.broadcasted_iota(jnp.int32, (count, count), 0)
    in_row = lax.broadcasted_iota(jnp.int32, (count, count), 1)
    stay = chosen == level
    same = jnp.where(in_row == out_row, 1, 0)
    pairs = jnp.where(in_row // 2 == out_row, weights_of(live, in_row, group), 0)
    mix = jnp.where(stay, same, pairs)
    total = weights_of(live, lax.broadcasted_iota(jnp.int32, (count, 1), 0), 2 * group)
    total = jnp.where(stay, 1, jnp.maximum(total, 1))
    summed = jnp.dot(
        mix.astype(jnp.float32).astype(jnp.bfloat16), values, preferred_element_type=jnp.float32
    )
    return (summed / total.astype(jnp.float32)).astype(jnp.bfloat16)


def attend_kernel(keep_ref, level_ref, live_ref, q_ref, own_ref, *rest):
    far_refs, out_ref, kv_ref, bias_ref = rest[:-3], rest[-3], rest[-2], rest[-1]
    tokens, width = q_ref.shape
    frames = live_ref.shape[0]
    frame = lax.axis_index("frames")
    own_live = live_ref[frame]

    def bias_row(live, count, group, active):
        weight = weights_of(live, lax.broadcasted_iota(jnp.int32, (8, count), 1), group)
        logs = jnp.log(jnp.maximum(weight, 1).astype(jnp.float32)) * LOG2E
        return jnp.where((weight > 0) & active, logs, FLOOR)

    kv_ref[0:tokens, :] = own_ref[...]
    bias_ref[:, 0:tokens] = bias_row(own_live, tokens, 1, True)
    at = tokens
    for number, far_ref in enumerate(far_refs):
        level, sign = number // 2, 1 - 2 * (number % 2)
        count = far_ref.shape[0]
        source = frame + sign * 2**level
        inside = (source >= 0) & (source < frames)
        source = jnp.clip(source, 0, frames - 1)
        chosen = level_ref[0, source]
        live = live_ref[source]
        known = (chosen == level) | (chosen == level + 1)
        active = inside & (keep_ref[0, source] == 1) & known
        group = jnp.where(chosen == level, 2**level, 2 ** (level + 1))
        kv_ref[at : at + count, :] = selected(far_ref[...], live, level, chosen)
        bias_ref[:, at : at + count] = bias_row(live, count, group, active)
        at += count
    bias = bias_ref[0:1, :]
    alive = lax.broadcasted_iota(jnp.int32, (tokens, 1), 0) < own_live
    for head in range(width // HDIM):
        columns = slice(head * HDIM, (head + 1) * HDIM)
        scores = lax.dot_general(
            q_ref[:, columns],
            kv_ref[:, columns],
            (((1,), (1,)), ((), ())),
            preferred_element_type=jnp.float32,
        )
        scores = scores * (LOG2E / math.sqrt(HDIM)) + bias
        probs = jnp.exp2(scores - jnp.max(scores, axis=1, keepdims=True))
        denominator = jnp.sum(probs, axis=1, keepdims=True)
        numerator = jnp.dot(
            probs.astype(jnp.bfloat16),
            kv_ref[:, width + head * HDIM : width + (head + 1) * HDIM],
            preferred_element_type=jnp.float32,
        )
        result = jnp.where(alive, numerator / denominator, 0.0)
        out_ref[:, columns] = result.astype(jnp.bfloat16)


def shards(query_in, key_in, value_in, query_gain, key_gain, keep_flags, pool_levels, live_counts):
    rows, features = query_in.shape
    parts = lax.axis_size("heads")
    frames = lax.axis_size("frames")
    tokens = rows * parts
    width = features // parts
    vmem = pl.BlockSpec(memory_space=pltpu.VMEM)
    smem = pl.BlockSpec(memory_space=pltpu.SMEM)
    params = pltpu.CompilerParams(vmem_limit_bytes=32 * 2**20)
    bf16 = jnp.bfloat16

    packed, query_parts = pl.pallas_call(
        prepare_kernel,
        out_shape=(
            jax.ShapeDtypeStruct((parts, rows, 2 * width), bf16),
            jax.ShapeDtypeStruct((parts, rows, width), bf16),
        ),
        in_specs=[vmem] * 6,
        out_specs=(vmem, vmem),
        compiler_params=params,
        name="prepare",
    )(
        query_in,
        key_in,
        value_in,
        query_gain.reshape(1, features),
        key_gain.reshape(1, features),
        jnp.asarray(frequency_rows()),
    )
    own = lax.all_to_all(packed, "heads", split_axis=0, concat_axis=0, tiled=True)
    own = own.reshape(tokens, 2 * width)
    query = lax.all_to_all(query_parts, "heads", split_axis=0, concat_axis=0, tiled=True)
    query = query.reshape(tokens, width)

    one, two = pl.pallas_call(
        pool_kernel,
        out_shape=(
            jax.ShapeDtypeStruct((tokens // 2, 2 * width), bf16),
            jax.ShapeDtypeStruct((tokens // 4, 2 * width), bf16),
        ),
        in_specs=[smem, vmem],
        out_specs=(vmem, vmem),
        compiler_params=params,
        name="pool",
    )(live_counts, own)

    far = []
    for level, rows_out in enumerate((own, one, two)):
        for sign in (1, -1):
            by = sign * 2**level
            pairs = [(i, i - by) for i in range(frames) if 0 <= i - by < frames]
            far.append(lax.ppermute(rows_out, "frames", pairs))

    count = tokens + sum(x.shape[0] for x in far)
    attended = pl.pallas_call(
        attend_kernel,
        out_shape=jax.ShapeDtypeStruct((tokens, width), bf16),
        in_specs=[smem] * 3 + [vmem] * (2 + len(far)),
        out_specs=vmem,
        scratch_shapes=[
            pltpu.VMEM((count, 2 * width), bf16),
            pltpu.VMEM((8, count), jnp.float32),
        ],
        compiler_params=params,
        name="attend",
    )(keep_flags, pool_levels, live_counts, query, own, *far)
    return lax.all_to_all(attended, "heads", split_axis=0, concat_axis=1, tiled=True)


def solution(mesh):
    placed = (
        P(("frames", "heads"), None),
        P(("frames", "heads"), None),
        P(("frames", "heads"), None),
        P(),
        P(),
        P("frames", None),
        P("frames", None),
        P(),
    )
    return jax.shard_map(
        shards, mesh=mesh, in_specs=placed, out_specs=P(("frames", "heads"), None), check_vma=False
    )
```

```python
import math

import jax
import jax.numpy as jnp
import numpy as np
from jax import lax
from jax.experimental import pallas as pl
from jax.experimental.pallas import tpu as pltpu
from jax.sharding import PartitionSpec as P

HDIM = 128
PW = 32
LEVELS = 3
EPSILON = 1e-06
FLOOR = -1e30
LOG2E = math.log2(math.e)


def frequency_rows():
    half = HDIM // 2
    third = half // 3
    lead = half - 2 * third
    rows = np.zeros((8, HDIM), np.float64)
    for lane in range(HDIM):
        i = lane // 2
        if i < lead:
            rows[0, lane] = 10000.0 ** (-i / lead)
        elif i < lead + third:
            rows[1, lane] = 10000.0 ** (-(i - lead) / third)
        else:
            rows[2, lane] = 10000.0 ** (-(i - lead - third) / third)
    return rows.astype(np.float32)


def prepare_kernel(
    q_hbm, k_hbm, v_hbm, qg_hbm, kg_hbm, freq_hbm, kv_ref, qo_ref,
    q_ref, k_ref, qg_ref, kg_ref, freq_ref, arrived, placed,
):
    rows, width = q_ref.shape
    parts, _, part_width = qo_ref.shape
    copies = [
        pltpu.make_async_copy(source, target, arrived.at[number])
        for number, (source, target) in enumerate(
            (
                (k_hbm, k_ref),
                (freq_hbm, freq_ref),
                (kg_hbm, kg_ref),
                (q_hbm, q_ref),
                (qg_hbm, qg_ref),
            )
        )
    ]
    copies += [
        pltpu.make_async_copy(
            v_hbm.at[:, part * part_width : (part + 1) * part_width],
            kv_ref.at[part, :, part_width:],
            placed.at[part],
        )
        for part in range(parts)
    ]
    for copy in copies:
        copy.start()
    frame = lax.axis_index("frames")
    first = lax.axis_index("heads") * rows
    token = first + lax.broadcasted_iota(jnp.int32, (rows, HDIM), 0)
    lane = lax.broadcasted_iota(jnp.int32, (rows, HDIM), 1)
    even = lane % 2 == 0
    for copy in copies[:3]:
        copy.wait()
    freq = freq_ref[...]
    angles = (
        frame.astype(jnp.float32) * freq[0:1]
        + (token // PW).astype(jnp.float32) * freq[1:2]
        + (token % PW).astype(jnp.float32) * freq[2:3]
    )
    cosine = jnp.cos(angles)
    sine = jnp.sin(angles)
    sine = jnp.where(even, -sine, sine)

    def turn(x_ref, gain_ref, out_ref):
        floats = x_ref[...].astype(jnp.float32)
        inverse = lax.rsqrt(jnp.mean(floats * floats, axis=1, keepdims=True) + EPSILON)
        gain = gain_ref[...]
        for head in range(width // HDIM):
            at = head * HDIM
            scaled = floats[:, at : at + HDIM] * inverse * gain[:, at : at + HDIM]
            partner = jnp.where(
                even, pltpu.roll(scaled, HDIM - 1, 1), pltpu.roll(scaled, 1, 1)
            )
            turned = (scaled * cosine + partner * sine).astype(jnp.bfloat16)
            part, offset = at // part_width, at % part_width
            out_ref[part, :, offset : offset + HDIM] = turned

    turn(k_ref, kg_ref, kv_ref)
    for copy in copies[3:5]:
        copy.wait()
    turn(q_ref, qg_ref, qo_ref)
    for copy in copies[5:]:
        copy.wait()


def partner_of(frame, distance, kind):
    if kind == 0:
        return frame ^ distance
    return ((frame + distance) ^ distance) - distance


def weights_of(live, index, group):
    return jnp.clip(live - index * group, 0, group)


def pooled(values, live, level):
    count = values.shape[0]
    half = count // 2
    group = 2**level
    out_row = lax.broadcasted_iota(jnp.int32, (half, count), 0)
    in_row = lax.broadcasted_iota(jnp.int32, (half, count), 1)
    mix = jnp.where(in_row // 2 == out_row, weights_of(live, in_row, group), 0)
    total = weights_of(live, lax.broadcasted_iota(jnp.int32, (half, 1), 0), 2 * group)
    summed = jnp.dot(
        mix.astype(jnp.float32).astype(jnp.bfloat16), values, preferred_element_type=jnp.float32
    )
    return (summed / jnp.maximum(total, 1).astype(jnp.float32)).astype(jnp.bfloat16)


def pool_kernel(live_ref, kv_ref, one_ref, two_ref):
    live = live_ref[lax.axis_index("frames")]
    one = pooled(kv_ref[...], live, 0)
    one_ref[...] = one
    two_ref[...] = pooled(one, live, 1)


def selected(values, live, level, chosen):
    count = values.shape[0]
    group = 2**level
    out_row = lax.broadcasted_iota(jnp.int32, (count, count), 0)
    in_row = lax.broadcasted_iota(jnp.int32, (count, count), 1)
    stay = chosen == level
    same = jnp.where(in_row == out_row, 1, 0)
    pairs = jnp.where(in_row // 2 == out_row, weights_of(live, in_row, group), 0)
    mix = jnp.where(stay, same, pairs)
    total = weights_of(live, lax.broadcasted_iota(jnp.int32, (count, 1), 0), 2 * group)
    total = jnp.where(stay, 1, jnp.maximum(total, 1))
    summed = jnp.dot(
        mix.astype(jnp.float32).astype(jnp.bfloat16), values, preferred_element_type=jnp.float32
    )
    return (summed / total.astype(jnp.float32)).astype(jnp.bfloat16)


def attend_kernel(keep_ref, level_ref, live_ref, q_ref, own_ref, *rest):
    far_refs, out_ref, kv_ref, bias_ref = rest[:-3], rest[-3], rest[-2], rest[-1]
    tokens, width = q_ref.shape
    frames = live_ref.shape[0]
    frame = lax.axis_index("frames")
    own_live = live_ref[frame]

    def bias_row(live, count, group, active):
        weight = weights_of(live, lax.broadcasted_iota(jnp.int32, (8, count), 1), group)
        logs = jnp.log(jnp.maximum(weight, 1).astype(jnp.float32)) * LOG2E
        return jnp.where((weight > 0) & active, logs, FLOOR)

    kv_ref[0:tokens, :] = own_ref[...]
    bias_ref[:, 0:tokens] = bias_row(own_live, tokens, 1, True)
    at = tokens
    for number, far_ref in enumerate(far_refs):
        level, kind = number // 2, number % 2
        count = far_ref.shape[0]
        source = partner_of(frame, 2**level, kind)
        inside = (source >= 0) & (source < frames)
        source = jnp.clip(source, 0, frames - 1)
        chosen = level_ref[0, source]
        live = live_ref[source]
        known = (chosen == level) | (chosen == level + 1)
        active = inside & (keep_ref[0, source] == 1) & known
        group = jnp.where(chosen == level, 2**level, 2 ** (level + 1))
        kv_ref[at : at + count, :] = selected(far_ref[...], live, level, chosen)
        bias_ref[:, at : at + count] = bias_row(live, count, group, active)
        at += count
    bias = bias_ref[0:1, :]
    alive = lax.broadcasted_iota(jnp.int32, (tokens, 1), 0) < own_live
    for head in range(width // HDIM):
        columns = slice(head * HDIM, (head + 1) * HDIM)
        scores = lax.dot_general(
            q_ref[:, columns],
            kv_ref[:, columns],
            (((1,), (1,)), ((), ())),
            preferred_element_type=jnp.float32,
        )
        scores = scores * (LOG2E / math.sqrt(HDIM)) + bias
        probs = jnp.exp2(scores - jnp.max(scores, axis=1, keepdims=True))
        denominator = jnp.sum(probs, axis=1, keepdims=True)
        numerator = jnp.dot(
            probs.astype(jnp.bfloat16),
            kv_ref[:, width + head * HDIM : width + (head + 1) * HDIM],
            preferred_element_type=jnp.float32,
        )
        result = jnp.where(alive, numerator / denominator, 0.0)
        out_ref[:, columns] = result.astype(jnp.bfloat16)


def shards(query_in, key_in, value_in, query_gain, key_gain, keep_flags, pool_levels, live_counts):
    rows, features = query_in.shape
    parts = lax.axis_size("heads")
    frames = lax.axis_size("frames")
    tokens = rows * parts
    width = features // parts
    vmem = pl.BlockSpec(memory_space=pltpu.VMEM)
    smem = pl.BlockSpec(memory_space=pltpu.SMEM)
    params = pltpu.CompilerParams(vmem_limit_bytes=32 * 2**20)
    alone = pltpu.CompilerParams(vmem_limit_bytes=60 * 2**20)
    bf16 = jnp.bfloat16

    packed, query_parts = pl.pallas_call(
        prepare_kernel,
        out_shape=(
            jax.ShapeDtypeStruct((parts, rows, 2 * width), bf16),
            jax.ShapeDtypeStruct((parts, rows, width), bf16),
        ),
        in_specs=[pl.BlockSpec(memory_space=pl.ANY)] * 6,
        out_specs=(vmem, vmem),
        scratch_shapes=[
            pltpu.VMEM((rows, features), bf16),
            pltpu.VMEM((rows, features), bf16),
            pltpu.VMEM((1, features), jnp.float32),
            pltpu.VMEM((1, features), jnp.float32),
            pltpu.VMEM((8, HDIM), jnp.float32),
            pltpu.SemaphoreType.DMA((5,)),
            pltpu.SemaphoreType.DMA((parts,)),
        ],
        compiler_params=alone,
        name="prepare",
    )(
        query_in,
        key_in,
        value_in,
        query_gain.reshape(1, features),
        key_gain.reshape(1, features),
        jnp.asarray(frequency_rows()),
    )
    own = lax.all_to_all(packed, "heads", split_axis=0, concat_axis=0, tiled=True)
    own = own.reshape(tokens, 2 * width)
    query = lax.all_to_all(query_parts, "heads", split_axis=0, concat_axis=0, tiled=True)
    query = query.reshape(tokens, width)

    one, two = pl.pallas_call(
        pool_kernel,
        out_shape=(
            jax.ShapeDtypeStruct((tokens // 2, 2 * width), bf16),
            jax.ShapeDtypeStruct((tokens // 4, 2 * width), bf16),
        ),
        in_specs=[smem, vmem],
        out_specs=(vmem, vmem),
        compiler_params=params,
        name="pool",
    )(live_counts, own)

    def exchanged(values, distance, kind):
        pairs = []
        for frame in range(frames):
            other = partner_of(frame, distance, kind)
            for part in range(parts):
                here = frame * parts + part
                if 0 <= other < frames:
                    pairs.append((here, other * parts + part))
                else:
                    pairs.append((here, frame * parts + (part ^ 1)))
        return lax.ppermute(values, ("frames", "heads"), pairs)

    far = []
    for level, values in enumerate((own, one, two)):
        for kind in (0, 1):
            if far:
                values, _ = lax.optimization_barrier((values, far[0])) if level == 2 and kind == 1 else (values, 0)
            far.append(exchanged(values, 2**level, kind))

    count = tokens + sum(x.shape[0] for x in far)
    attended = pl.pallas_call(
        attend_kernel,
        out_shape=jax.ShapeDtypeStruct((tokens, width), bf16),
        in_specs=[smem] * 3 + [vmem] * (2 + len(far)),
        out_specs=vmem,
        scratch_shapes=[
            pltpu.VMEM((count, 2 * width), bf16),
            pltpu.VMEM((8, count), jnp.float32),
        ],
        compiler_params=params,
        name="attend",
    )(keep_flags, pool_levels, live_counts, query, own, *far)
    return lax.all_to_all(attended, "heads", split_axis=0, concat_axis=1, tiled=True)


def solution(mesh):
    placed = (
        P(("frames", "heads"), None),
        P(("frames", "heads"), None),
        P(("frames", "heads"), None),
        P(),
        P(),
        P("frames", None),
        P("frames", None),
        P(),
    )
    return jax.shard_map(
        shards, mesh=mesh, in_specs=placed, out_specs=P(("frames", "heads"), None), check_vma=False
    )
```

```python
import math

import jax
import jax.numpy as jnp
import numpy as np
from jax import lax
from jax.experimental import pallas as pl
from jax.experimental.pallas import tpu as pltpu
from jax.sharding import PartitionSpec as P

HDIM = 128
PW = 32
LEVELS = 3
EPSILON = 1e-06
FLOOR = -1e30
LOG2E = math.log2(math.e)


def frequency_rows():
    half = HDIM // 2
    third = half // 3
    lead = half - 2 * third
    rows = np.zeros((8, HDIM), np.float64)
    for lane in range(HDIM):
        i = lane // 2
        if i < lead:
            rows[0, lane] = 10000.0 ** (-i / lead)
        elif i < lead + third:
            rows[1, lane] = 10000.0 ** (-(i - lead) / third)
        else:
            rows[2, lane] = 10000.0 ** (-(i - lead - third) / third)
    return rows.astype(np.float32)


def rotary_tables(rows, freq):
    frame = lax.axis_index("frames")
    token = lax.axis_index("heads") * rows + lax.broadcasted_iota(jnp.int32, (rows, HDIM), 0)
    even = lax.broadcasted_iota(jnp.int32, (rows, HDIM), 1) % 2 == 0
    angles = (
        frame.astype(jnp.float32) * freq[0:1]
        + (token // PW).astype(jnp.float32) * freq[1:2]
        + (token % PW).astype(jnp.float32) * freq[2:3]
    )
    sine = jnp.sin(angles)
    return jnp.cos(angles), jnp.where(even, -sine, sine), even


def block_bases(count, width):
    own_part = lax.axis_index("heads")
    return [pl.multiple_of((own_part ^ step) * width, width) for step in range(count)]


def turn(x_ref, gain_ref, tables, stores, part_width):
    cosine, sine, even = tables
    floats = x_ref[...].astype(jnp.float32)
    inverse = lax.rsqrt(jnp.mean(floats * floats, axis=1, keepdims=True) + EPSILON)
    for base, store in zip(block_bases(len(stores), part_width), stores):
        for offset in range(0, part_width, HDIM):
            at = pl.ds(pl.multiple_of(base + offset, HDIM), HDIM)
            scaled = x_ref[:, at].astype(jnp.float32) * inverse * gain_ref[:, at]
            partner = jnp.where(even, pltpu.roll(scaled, HDIM - 1, 1), pltpu.roll(scaled, 1, 1))
            store(offset, (scaled * cosine + partner * sine).astype(jnp.bfloat16))


def store_in(ref):
    def store(offset, values):
        ref[:, offset : offset + HDIM] = values

    return store


def prepare_kernel(live_ref, k_hbm, v_hbm, kg_hbm, freq_hbm, q_hbm, qg_hbm, *rest):
    (*block_refs, early_ref, qo_ref, k_ref, kg_ref, freq_ref, q_ref, qg_ref, arrived, placed) = rest
    rows, width = k_ref.shape
    part_width = width // len(block_refs)
    bases = block_bases(len(block_refs), part_width)
    copies = [
        pltpu.make_async_copy(source, target, arrived.at[number])
        for number, (source, target) in enumerate(
            (
                (freq_hbm, freq_ref),
                (k_hbm, k_ref),
                (kg_hbm, kg_ref),
                (q_hbm, q_ref),
                (qg_hbm, qg_ref),
            )
        )
    ]
    copies += [
        pltpu.make_async_copy(
            v_hbm.at[:, pl.ds(base, part_width)],
            block_ref.at[:, part_width:],
            placed.at[step],
        )
        for step, (base, block_ref) in enumerate(zip(bases, block_refs))
    ]
    for copy in copies:
        copy.start()
    copies[0].wait()
    tables = rotary_tables(rows, freq_ref[...])
    copies[1].wait()
    copies[2].wait()
    turn(k_ref, kg_ref, tables, [store_in(ref) for ref in block_refs], part_width)
    for copy in copies[3:]:
        copy.wait()
    live = live_ref[lax.axis_index("frames")] - lax.axis_index("heads") * rows
    for base, block_ref in zip(bases, block_refs):
        two = pooled_floats(pooled(block_ref[...], live, 0), live, 1)
        both = jnp.concatenate([two[:, :part_width], two[:, part_width:]], axis=0)
        early_ref[:, pl.ds(base, part_width)] = both.astype(jnp.bfloat16)
    turn(
        q_ref,
        qg_ref,
        tables,
        [store_in(qo_ref.at[step]) for step in range(len(block_refs))],
        part_width,
    )


def source_of(frame, slot):
    odd = frame % 2
    if slot == "cross":
        return ((frame + 1) ^ 1) - 1
    if slot == "chip":
        return frame ^ 1
    if slot == "ahead":
        return frame + 4 * odd - 2
    if slot == "handed":
        return frame - 4 * odd + 2
    if slot == "four":
        return frame ^ 4
    return ((frame + 4) ^ 4) - 4


def weights_of(live, index, group):
    return jnp.clip(live - index * group, 0, group)


def pooled_floats(values, live, level):
    count = values.shape[0]
    half = count // 2
    group = 2**level
    out_row = lax.broadcasted_iota(jnp.int32, (half, count), 0)
    in_row = lax.broadcasted_iota(jnp.int32, (half, count), 1)
    mix = jnp.where(in_row // 2 == out_row, weights_of(live, in_row, group), 0)
    total = weights_of(live, lax.broadcasted_iota(jnp.int32, (half, 1), 0), 2 * group)
    summed = jnp.dot(
        mix.astype(jnp.float32).astype(jnp.bfloat16), values, preferred_element_type=jnp.float32
    )
    return summed / jnp.maximum(total, 1).astype(jnp.float32)


def pooled(values, live, level):
    return pooled_floats(values, live, level).astype(jnp.bfloat16)


def assemble_kernel(*refs):
    block_refs, own_ref = refs[:-1], refs[-1]
    rows = block_refs[0].shape[0]
    for first, block_ref in zip(block_bases(len(block_refs), rows), block_refs):
        own_ref[pl.ds(first, rows), :] = block_ref[...]


def pool_kernel(live_ref, own_ref, one_ref):
    one_ref[...] = pooled(own_ref[...], live_ref[lax.axis_index("frames")], 0)


def pool_cross_kernel(live_ref, far_ref, out_ref):
    source = source_of(lax.axis_index("frames"), "cross")
    source = jnp.clip(source, 0, live_ref.shape[0] - 1)
    out_ref[...] = pooled(far_ref[...], live_ref[source], 0)


def pack_kernel(four_ref, back_ref, q_ref, *out_refs):
    parts, rows, width = q_ref.shape
    count = four_ref.shape[0]
    for step, (base, out_ref) in enumerate(zip(block_bases(parts, width), out_refs)):
        out_ref[:rows, :] = q_ref[step]
        out_ref[rows : rows + count, :] = four_ref[:, pl.ds(base, width)]
        out_ref[rows + count :, :] = back_ref[:, pl.ds(base, width)]


def selection(in_index, valid, shape, live, level, chosen):
    out_row = lax.broadcasted_iota(jnp.int32, shape, 0)
    group = 2**level
    stay = chosen == level
    same = jnp.where(in_index == out_row, 1, 0)
    pairs = jnp.where(in_index // 2 == out_row, weights_of(live, in_index, group), 0)
    mix = jnp.where(valid, jnp.where(stay, same, pairs), 0)
    total = weights_of(live, lax.broadcasted_iota(jnp.int32, (shape[0], 1), 0), 2 * group)
    total = jnp.where(stay, 1, jnp.maximum(total, 1))
    return mix.astype(jnp.float32).astype(jnp.bfloat16), total.astype(jnp.float32)


def mixed(mix, values, total):
    summed = jnp.dot(mix, values, preferred_element_type=jnp.float32)
    return (summed / total).astype(jnp.bfloat16)


SLOTS = ("cross", "chip", "ahead", "handed", "four", "back")


def attend_kernel(keep_ref, level_ref, live_ref, own_ref, *rest):
    (*refs, out_ref, q_ref, kv_ref, bias_ref, early_ref) = rest
    far_refs, packed_refs = refs[:4], refs[4:]
    tokens, width = q_ref.shape
    frames = live_ref.shape[0]
    parts = len(packed_refs)
    rows = tokens // parts
    early_rows = (packed_refs[0].shape[0] - rows) // 2
    groups = early_rows // 2
    frame = lax.axis_index("frames")
    own_live = live_ref[frame]

    def bias_row(live, count, group, active):
        weight = weights_of(live, lax.broadcasted_iota(jnp.int32, (8, count), 1), group)
        logs = jnp.log(jnp.maximum(weight, 1).astype(jnp.float32)) * LOG2E
        return jnp.where((weight > 0) & active, logs, FLOOR)

    for first, packed_ref in zip(block_bases(parts, rows), packed_refs):
        q_ref[pl.ds(first, rows), :] = packed_ref[:rows, :]
    kv_ref[0:tokens, :] = own_ref[...]
    bias_ref[:, 0:tokens] = bias_row(own_live, tokens, 1, True)
    at = tokens
    for number, slot in enumerate(SLOTS):
        level, kind = number // 2, number % 2
        count = tokens >> level
        source = source_of(frame, slot)
        inside = (source >= 0) & (source < frames)
        source = jnp.clip(source, 0, frames - 1)
        chosen = level_ref[0, source]
        live = live_ref[source]
        known = (chosen == level) | (chosen == level + 1)
        active = inside & (keep_ref[0, source] == 1) & known
        group = jnp.where(chosen == level, 2**level, 2 ** (level + 1))
        bias_ref[:, at : at + count] = bias_row(live, count, group, active)
        if number < len(far_refs):
            in_index = lax.broadcasted_iota(jnp.int32, (count, count), 1)
            mix, total = selection(in_index, True, (count, count), live, level, chosen)
            kv_ref[at : at + count, :] = mixed(mix, far_refs[number][...], total)
        else:
            skip = rows + kind * early_rows
            for step, packed_ref in enumerate(packed_refs):
                early_ref[kind, step * early_rows : (step + 1) * early_rows, :] = packed_ref[
                    skip : skip + early_rows, :
                ]
            shape = (count, parts * early_rows)
            in_row = lax.broadcasted_iota(jnp.int32, shape, 1)
            inner = in_row % early_rows
            part = (in_row // early_rows) ^ lax.axis_index("heads")
            in_index = part * groups + inner % groups
            for half in range(2):
                valid = inner // groups == half
                mix, total = selection(in_index, valid, shape, live, level, chosen)
                kv_ref[at : at + count, half * width : (half + 1) * width] = mixed(
                    mix, early_ref[kind], total
                )
        at += count
    bias = bias_ref[0:1, :]
    alive = lax.broadcasted_iota(jnp.int32, (tokens, 1), 0) < own_live
    for head in range(width // HDIM):
        columns = slice(head * HDIM, (head + 1) * HDIM)
        scores = lax.dot_general(
            q_ref[:, columns],
            kv_ref[:, columns],
            (((1,), (1,)), ((), ())),
            preferred_element_type=jnp.float32,
        )
        scores = scores * (LOG2E / math.sqrt(HDIM)) + bias
        probs = jnp.exp2(scores - jnp.max(scores, axis=1, keepdims=True))
        denominator = jnp.sum(probs, axis=1, keepdims=True)
        numerator = jnp.dot(
            probs.astype(jnp.bfloat16),
            kv_ref[:, width + head * HDIM : width + (head + 1) * HDIM],
            preferred_element_type=jnp.float32,
        )
        result = jnp.where(alive, numerator / denominator, 0.0)
        out_ref[:, columns] = result.astype(jnp.bfloat16)


def shards(query_in, key_in, value_in, query_gain, key_gain, keep_flags, pool_levels, live_counts):
    rows, features = query_in.shape
    parts = lax.axis_size("heads")
    frames = lax.axis_size("frames")
    tokens = rows * parts
    width = features // parts
    vmem = pl.BlockSpec(memory_space=pltpu.VMEM)
    smem = pl.BlockSpec(memory_space=pltpu.SMEM)
    params = pltpu.CompilerParams(vmem_limit_bytes=32 * 2**20)
    alone = pltpu.CompilerParams(vmem_limit_bytes=60 * 2**20)
    bf16 = jnp.bfloat16

    anywhere = pl.BlockSpec(memory_space=pl.ANY)
    early_rows = 2 * rows >> (LEVELS - 1)
    floats = jnp.float32
    freq = jnp.asarray(frequency_rows())

    def array(*shape):
        return jax.ShapeDtypeStruct(shape, bf16)

    *blocks, early, query_blocks = pl.pallas_call(
        prepare_kernel,
        out_shape=[array(rows, 2 * width)] * parts
        + [array(early_rows, features), array(parts, rows, width)],
        in_specs=[smem] + [anywhere] * 6,
        out_specs=[vmem] * (parts + 2),
        scratch_shapes=[
            pltpu.VMEM((rows, features), bf16),
            pltpu.VMEM((1, features), floats),
            pltpu.VMEM((8, HDIM), floats),
            pltpu.VMEM((rows, features), bf16),
            pltpu.VMEM((1, features), floats),
            pltpu.SemaphoreType.DMA((5,)),
            pltpu.SemaphoreType.DMA((parts,)),
        ],
        compiler_params=alone,
        name="prepare",
    )(
        live_counts,
        key_in,
        value_in,
        key_gain.reshape(1, features),
        freq,
        query_in,
        query_gain.reshape(1, features),
    )

    def permuted(values, slot):
        pairs = []
        for frame in range(frames):
            source = source_of(frame, slot)
            for part in range(parts):
                there = frame * parts + part
                if 0 <= source < frames:
                    pairs.append((source * parts + part, there))
                elif slot == "ahead":
                    pairs.append(((frame ^ 1) * parts + part, there))
                else:
                    pairs.append((frame * parts + (part ^ 1), there))
        return lax.ppermute(values, ("frames", "heads"), pairs)

    def over_parts(blocks):
        return [blocks[0]] + [
            lax.ppermute(blocks[step], "heads", [(i, i ^ step) for i in range(parts)])
            for step in range(1, parts)
        ]

    blocks = over_parts(blocks)
    four, back = permuted(early, "four"), permuted(early, "back")
    own = pl.pallas_call(
        assemble_kernel,
        out_shape=array(tokens, 2 * width),
        in_specs=[vmem] * parts,
        out_specs=vmem,
        compiler_params=params,
        name="assemble",
    )(*blocks)
    own, four, back = lax.optimization_barrier((own, four, back))
    cross, chip = permuted(own, "cross"), permuted(own, "chip")
    one = pl.pallas_call(
        pool_kernel,
        out_shape=array(tokens // 2, 2 * width),
        in_specs=[smem, vmem],
        out_specs=vmem,
        compiler_params=params,
        name="pool",
    )(live_counts, own)
    ahead = permuted(one, "ahead")
    packed = pl.pallas_call(
        pack_kernel,
        out_shape=[array(rows + 2 * early_rows, width)] * parts,
        in_specs=[vmem] * 3,
        out_specs=[vmem] * parts,
        compiler_params=params,
        name="pack",
    )(four, back, query_blocks)
    packed = over_parts(packed)

    cross, *packed = lax.optimization_barrier((cross, *packed))
    cross_one = pl.pallas_call(
        pool_cross_kernel,
        out_shape=jax.ShapeDtypeStruct((tokens // 2, 2 * width), bf16),
        in_specs=[smem, vmem],
        out_specs=vmem,
        compiler_params=params,
        name="pool_cross",
    )(live_counts, cross)
    far = (cross, chip, ahead, permuted(cross_one, "chip"))
    count = tokens + 2 * sum(tokens >> level for level in range(LEVELS))
    attended = pl.pallas_call(
        attend_kernel,
        out_shape=jax.ShapeDtypeStruct((tokens, width), bf16),
        in_specs=[smem] * 3 + [vmem] * (1 + len(far) + parts),
        out_specs=vmem,
        scratch_shapes=[
            pltpu.VMEM((tokens, width), bf16),
            pltpu.VMEM((count, 2 * width), bf16),
            pltpu.VMEM((8, count), jnp.float32),
            pltpu.VMEM((2, parts * early_rows, width), bf16),
        ],
        compiler_params=params,
        name="attend",
    )(keep_flags, pool_levels, live_counts, own, *far, *packed)
    return lax.all_to_all(attended, "heads", split_axis=0, concat_axis=1, tiled=True)


def solution(mesh):
    placed = (
        P(("frames", "heads"), None),
        P(("frames", "heads"), None),
        P(("frames", "heads"), None),
        P(),
        P(),
        P("frames", None),
        P("frames", None),
        P(),
    )
    return jax.shard_map(
        shards, mesh=mesh, in_specs=placed, out_specs=P(("frames", "heads"), None), check_vma=False
    )
```

```python
import math

import jax
import jax.numpy as jnp
import numpy as np
from jax import lax
from jax.experimental import pallas as pl
from jax.experimental.pallas import tpu as pltpu
from jax.sharding import PartitionSpec as P

HDIM = 128
PW = 32
LEVELS = 3
EPSILON = 1e-06
FLOOR = -1e30
LOG2E = math.log2(math.e)


def frequency_rows():
    half = HDIM // 2
    third = half // 3
    lead = half - 2 * third
    rows = np.zeros((8, HDIM), np.float64)
    for lane in range(HDIM):
        i = lane // 2
        if i < lead:
            rows[0, lane] = 10000.0 ** (-i / lead)
        elif i < lead + third:
            rows[1, lane] = 10000.0 ** (-(i - lead) / third)
        else:
            rows[2, lane] = 10000.0 ** (-(i - lead - third) / third)
    return rows.astype(np.float32)


def rotary_tables(rows, freq):
    frame = lax.axis_index("frames")
    token = lax.axis_index("heads") * rows + lax.broadcasted_iota(jnp.int32, (rows, HDIM), 0)
    even = lax.broadcasted_iota(jnp.int32, (rows, HDIM), 1) % 2 == 0
    angles = (
        frame.astype(jnp.float32) * freq[0:1]
        + (token // PW).astype(jnp.float32) * freq[1:2]
        + (token % PW).astype(jnp.float32) * freq[2:3]
    )
    sine = jnp.sin(angles)
    return jnp.cos(angles), jnp.where(even, -sine, sine), even


def steps_of(count):
    return (0, *range(count - 1, 0, -1))


def block_bases(count, width):
    own_part = lax.axis_index("heads")
    return [pl.multiple_of((own_part ^ step) * width, width) for step in steps_of(count)]


def turn(x_ref, gain_ref, tables, stores, part_width):
    cosine, sine, even = tables
    floats = x_ref[...].astype(jnp.float32)
    inverse = lax.rsqrt(jnp.mean(floats * floats, axis=1, keepdims=True) + EPSILON)
    for base, store in zip(block_bases(len(stores), part_width), stores):
        for offset in range(0, part_width, HDIM):
            at = pl.ds(pl.multiple_of(base + offset, HDIM), HDIM)
            scaled = x_ref[:, at].astype(jnp.float32) * inverse * gain_ref[:, at]
            partner = jnp.where(even, pltpu.roll(scaled, HDIM - 1, 1), pltpu.roll(scaled, 1, 1))
            store(offset, (scaled * cosine + partner * sine).astype(jnp.bfloat16))


def store_in(ref):
    def store(offset, values):
        ref[:, offset : offset + HDIM] = values

    return store


def prepare_kernel(live_ref, k_hbm, v_hbm, kg_hbm, freq_hbm, q_hbm, qg_hbm, *rest):
    (*block_refs, early_ref, qo_ref, k_ref, kg_ref, freq_ref, q_ref, qg_ref, arrived, placed) = rest
    rows, width = k_ref.shape
    part_width = width // len(block_refs)
    bases = block_bases(len(block_refs), part_width)
    copies = [
        pltpu.make_async_copy(source, target, arrived.at[number])
        for number, (source, target) in enumerate(
            (
                (freq_hbm, freq_ref),
                (k_hbm, k_ref),
                (kg_hbm, kg_ref),
                (q_hbm, q_ref),
                (qg_hbm, qg_ref),
            )
        )
    ]
    copies += [
        pltpu.make_async_copy(
            v_hbm.at[:, pl.ds(base, part_width)],
            block_ref.at[:, part_width:],
            placed.at[step],
        )
        for step, (base, block_ref) in enumerate(zip(bases, block_refs))
    ]
    for copy in copies:
        copy.start()
    copies[0].wait()
    tables = rotary_tables(rows, freq_ref[...])
    copies[1].wait()
    copies[2].wait()
    turn(k_ref, kg_ref, tables, [store_in(ref) for ref in block_refs], part_width)
    for copy in copies[3:]:
        copy.wait()
    live = live_ref[lax.axis_index("frames")] - lax.axis_index("heads") * rows
    for base, block_ref in zip(bases, block_refs):
        two = pooled_floats(pooled(block_ref[...], live, 0), live, 1)
        both = jnp.concatenate([two[:, :part_width], two[:, part_width:]], axis=0)
        early_ref[:, pl.ds(base, part_width)] = both.astype(jnp.bfloat16)
    turn(
        q_ref,
        qg_ref,
        tables,
        [store_in(qo_ref.at[step]) for step in range(len(block_refs))],
        part_width,
    )


def source_of(frame, slot):
    odd = frame % 2
    if slot == "cross":
        return ((frame + 1) ^ 1) - 1
    if slot == "chip":
        return frame ^ 1
    if slot == "ahead":
        return frame + 4 * odd - 2
    if slot == "handed":
        return frame - 4 * odd + 2
    if slot == "four":
        return frame ^ 4
    return ((frame + 4) ^ 4) - 4


def weights_of(live, index, group):
    return jnp.clip(live - index * group, 0, group)


def pooled_floats(values, live, level):
    count = values.shape[0]
    half = count // 2
    group = 2**level
    out_row = lax.broadcasted_iota(jnp.int32, (half, count), 0)
    in_row = lax.broadcasted_iota(jnp.int32, (half, count), 1)
    mix = jnp.where(in_row // 2 == out_row, weights_of(live, in_row, group), 0)
    total = weights_of(live, lax.broadcasted_iota(jnp.int32, (half, 1), 0), 2 * group)
    summed = jnp.dot(
        mix.astype(jnp.float32).astype(jnp.bfloat16), values, preferred_element_type=jnp.float32
    )
    return summed / jnp.maximum(total, 1).astype(jnp.float32)


def pooled(values, live, level):
    return pooled_floats(values, live, level).astype(jnp.bfloat16)


def assemble_kernel(*refs):
    block_refs, own_ref = refs[:-1], refs[-1]
    rows = block_refs[0].shape[0]
    for first, block_ref in zip(block_bases(len(block_refs), rows), block_refs):
        own_ref[pl.ds(first, rows), :] = block_ref[...]


def pool_kernel(live_ref, own_ref, one_ref):
    one_ref[...] = pooled(own_ref[...], live_ref[lax.axis_index("frames")], 0)


def pool_cross_kernel(live_ref, far_ref, out_ref):
    source = source_of(lax.axis_index("frames"), "cross")
    source = jnp.clip(source, 0, live_ref.shape[0] - 1)
    out_ref[...] = pooled(far_ref[...], live_ref[source], 0)


def pack_kernel(four_ref, back_ref, q_ref, *out_refs):
    parts, rows, width = q_ref.shape
    count = four_ref.shape[0]
    for step, (base, out_ref) in enumerate(zip(block_bases(parts, width), out_refs)):
        out_ref[:rows, :] = q_ref[step]
        out_ref[rows : rows + count, :] = four_ref[:, pl.ds(base, width)]
        out_ref[rows + count :, :] = back_ref[:, pl.ds(base, width)]


def selection(in_index, valid, shape, live, level, chosen):
    out_row = lax.broadcasted_iota(jnp.int32, shape, 0)
    group = 2**level
    stay = chosen == level
    same = jnp.where(in_index == out_row, 1, 0)
    pairs = jnp.where(in_index // 2 == out_row, weights_of(live, in_index, group), 0)
    mix = jnp.where(valid, jnp.where(stay, same, pairs), 0)
    total = weights_of(live, lax.broadcasted_iota(jnp.int32, (shape[0], 1), 0), 2 * group)
    total = jnp.where(stay, 1, jnp.maximum(total, 1))
    return mix.astype(jnp.float32).astype(jnp.bfloat16), total.astype(jnp.float32)


def mixed(mix, values, total):
    summed = jnp.dot(mix, values, preferred_element_type=jnp.float32)
    return (summed / total).astype(jnp.bfloat16)


SLOTS = ("cross", "chip", "ahead", "handed", "four", "back")


def attend_kernel(keep_ref, level_ref, live_ref, own_ref, *rest):
    (*refs, result_ref, q_ref, kv_ref, bias_ref, early_ref) = rest
    parts = (len(refs) - 4) // 2
    far_refs, packed_refs, out_refs = refs[:4], refs[4 : 4 + parts], refs[4 + parts :]
    tokens, width = q_ref.shape
    frames = live_ref.shape[0]
    rows = tokens // parts
    early_rows = (packed_refs[0].shape[0] - rows) // 2
    groups = early_rows // 2
    frame = lax.axis_index("frames")
    own_live = live_ref[frame]

    def bias_row(live, count, group, active):
        weight = weights_of(live, lax.broadcasted_iota(jnp.int32, (8, count), 1), group)
        logs = jnp.log(jnp.maximum(weight, 1).astype(jnp.float32)) * LOG2E
        return jnp.where((weight > 0) & active, logs, FLOOR)

    for first, packed_ref in zip(block_bases(parts, rows), packed_refs):
        q_ref[pl.ds(first, rows), :] = packed_ref[:rows, :]
    kv_ref[0:tokens, :] = own_ref[...]
    bias_ref[:, 0:tokens] = bias_row(own_live, tokens, 1, True)
    at = tokens
    for number, slot in enumerate(SLOTS):
        level, kind = number // 2, number % 2
        count = tokens >> level
        source = source_of(frame, slot)
        inside = (source >= 0) & (source < frames)
        source = jnp.clip(source, 0, frames - 1)
        chosen = level_ref[0, source]
        live = live_ref[source]
        known = (chosen == level) | (chosen == level + 1)
        active = inside & (keep_ref[0, source] == 1) & known
        group = jnp.where(chosen == level, 2**level, 2 ** (level + 1))
        bias_ref[:, at : at + count] = bias_row(live, count, group, active)
        if number < len(far_refs):
            in_index = lax.broadcasted_iota(jnp.int32, (count, count), 1)
            mix, total = selection(in_index, True, (count, count), live, level, chosen)
            kv_ref[at : at + count, :] = mixed(mix, far_refs[number][...], total)
        else:
            skip = rows + kind * early_rows
            for step, packed_ref in enumerate(packed_refs):
                early_ref[kind, step * early_rows : (step + 1) * early_rows, :] = packed_ref[
                    skip : skip + early_rows, :
                ]
            shape = (count, parts * early_rows)
            in_row = lax.broadcasted_iota(jnp.int32, shape, 1)
            inner = in_row % early_rows
            block = in_row // early_rows
            step = jnp.where(block == 0, 0, parts - block)
            part = step ^ lax.axis_index("heads")
            in_index = part * groups + inner % groups
            for half in range(2):
                valid = inner // groups == half
                mix, total = selection(in_index, valid, shape, live, level, chosen)
                kv_ref[at : at + count, half * width : (half + 1) * width] = mixed(
                    mix, early_ref[kind], total
                )
        at += count
    bias = bias_ref[0:1, :]
    alive = lax.broadcasted_iota(jnp.int32, (tokens, 1), 0) < own_live
    for head in range(width // HDIM):
        columns = slice(head * HDIM, (head + 1) * HDIM)
        scores = lax.dot_general(
            q_ref[:, columns],
            kv_ref[:, columns],
            (((1,), (1,)), ((), ())),
            preferred_element_type=jnp.float32,
        )
        scores = scores * (LOG2E / math.sqrt(HDIM)) + bias
        probs = jnp.exp2(scores - jnp.max(scores, axis=1, keepdims=True))
        denominator = jnp.sum(probs, axis=1, keepdims=True)
        numerator = jnp.dot(
            probs.astype(jnp.bfloat16),
            kv_ref[:, width + head * HDIM : width + (head + 1) * HDIM],
            preferred_element_type=jnp.float32,
        )
        result = jnp.where(alive, numerator / denominator, 0.0)
        result_ref[:, columns] = result.astype(jnp.bfloat16)
    for first, out_ref in zip(block_bases(parts, rows), out_refs):
        out_ref[...] = result_ref[pl.ds(first, rows), :]


def place_kernel(*refs):
    block_refs, (out_ref, placed) = refs[:-2], refs[-2:]
    width = block_refs[0].shape[1]
    copies = [
        pltpu.make_async_copy(block_ref, out_ref.at[:, pl.ds(base, width)], placed.at[step])
        for step, (base, block_ref) in enumerate(
            zip(block_bases(len(block_refs), width), block_refs)
        )
    ]
    for copy in copies:
        copy.start()
    for copy in copies:
        copy.wait()


def shards(query_in, key_in, value_in, query_gain, key_gain, keep_flags, pool_levels, live_counts):
    rows, features = query_in.shape
    parts = lax.axis_size("heads")
    frames = lax.axis_size("frames")
    tokens = rows * parts
    width = features // parts
    vmem = pl.BlockSpec(memory_space=pltpu.VMEM)
    smem = pl.BlockSpec(memory_space=pltpu.SMEM)
    params = pltpu.CompilerParams(vmem_limit_bytes=32 * 2**20)
    alone = pltpu.CompilerParams(vmem_limit_bytes=60 * 2**20)
    bf16 = jnp.bfloat16

    anywhere = pl.BlockSpec(memory_space=pl.ANY)
    early_rows = 2 * rows >> (LEVELS - 1)
    floats = jnp.float32
    freq = jnp.asarray(frequency_rows())

    def array(*shape):
        return jax.ShapeDtypeStruct(shape, bf16)

    *blocks, early, query_blocks = pl.pallas_call(
        prepare_kernel,
        out_shape=[array(rows, 2 * width)] * parts
        + [array(early_rows, features), array(parts, rows, width)],
        in_specs=[smem] + [anywhere] * 6,
        out_specs=[vmem] * (parts + 2),
        scratch_shapes=[
            pltpu.VMEM((rows, features), bf16),
            pltpu.VMEM((1, features), floats),
            pltpu.VMEM((8, HDIM), floats),
            pltpu.VMEM((rows, features), bf16),
            pltpu.VMEM((1, features), floats),
            pltpu.SemaphoreType.DMA((5,)),
            pltpu.SemaphoreType.DMA((parts,)),
        ],
        compiler_params=alone,
        name="prepare",
    )(
        live_counts,
        key_in,
        value_in,
        key_gain.reshape(1, features),
        freq,
        query_in,
        query_gain.reshape(1, features),
    )

    def permuted(values, slot):
        pairs = []
        for frame in range(frames):
            source = source_of(frame, slot)
            for part in range(parts):
                there = frame * parts + part
                if 0 <= source < frames:
                    pairs.append((source * parts + part, there))
                elif slot == "ahead":
                    pairs.append(((frame ^ 1) * parts + part, there))
                else:
                    pairs.append((frame * parts + (part ^ 1), there))
        return lax.ppermute(values, ("frames", "heads"), pairs)

    def over_parts(blocks):
        return [blocks[0]] + [
            lax.ppermute(block, "heads", [(i, i ^ step) for i in range(parts)])
            for step, block in zip(steps_of(parts)[1:], blocks[1:])
        ]

    blocks = over_parts(blocks)
    four, back = permuted(early, "four"), permuted(early, "back")
    own = pl.pallas_call(
        assemble_kernel,
        out_shape=array(tokens, 2 * width),
        in_specs=[vmem] * parts,
        out_specs=vmem,
        compiler_params=params,
        name="assemble",
    )(*blocks)
    own, four, back = lax.optimization_barrier((own, four, back))
    cross, chip = permuted(own, "cross"), permuted(own, "chip")
    one = pl.pallas_call(
        pool_kernel,
        out_shape=array(tokens // 2, 2 * width),
        in_specs=[smem, vmem],
        out_specs=vmem,
        compiler_params=params,
        name="pool",
    )(live_counts, own)
    ahead = permuted(one, "ahead")
    four, back, chip = lax.optimization_barrier((four, back, chip))
    packed = pl.pallas_call(
        pack_kernel,
        out_shape=[array(rows + 2 * early_rows, width)] * parts,
        in_specs=[vmem] * 3,
        out_specs=[vmem] * parts,
        compiler_params=params,
        name="pack",
    )(four, back, query_blocks)
    packed = over_parts(packed)

    cross, *packed = lax.optimization_barrier((cross, *packed))
    cross_one = pl.pallas_call(
        pool_cross_kernel,
        out_shape=jax.ShapeDtypeStruct((tokens // 2, 2 * width), bf16),
        in_specs=[smem, vmem],
        out_specs=vmem,
        compiler_params=params,
        name="pool_cross",
    )(live_counts, cross)
    far = (cross, chip, ahead, permuted(cross_one, "chip"))
    count = tokens + 2 * sum(tokens >> level for level in range(LEVELS))
    attended = pl.pallas_call(
        attend_kernel,
        out_shape=[array(rows, width)] * parts,
        in_specs=[smem] * 3 + [vmem] * (1 + len(far) + parts),
        out_specs=[vmem] * parts,
        scratch_shapes=[
            pltpu.VMEM((tokens, width), bf16),
            pltpu.VMEM((tokens, width), bf16),
            pltpu.VMEM((count, 2 * width), bf16),
            pltpu.VMEM((8, count), jnp.float32),
            pltpu.VMEM((2, parts * early_rows, width), bf16),
        ],
        compiler_params=params,
        name="attend",
    )(keep_flags, pool_levels, live_counts, own, *far, *packed)
    return pl.pallas_call(
        place_kernel,
        out_shape=array(rows, features),
        in_specs=[vmem] * parts,
        out_specs=anywhere,
        scratch_shapes=[pltpu.SemaphoreType.DMA((parts,))],
        compiler_params=params,
        name="place",
    )(*over_parts(attended))


def solution(mesh):
    placed = (
        P(("frames", "heads"), None),
        P(("frames", "heads"), None),
        P(("frames", "heads"), None),
        P(),
        P(),
        P("frames", None),
        P("frames", None),
        P(),
    )
    return jax.shard_map(
        shards, mesh=mesh, in_specs=placed, out_specs=P(("frames", "heads"), None), check_vma=False
    )
```

```python
import math

import jax
import jax.numpy as jnp
import numpy as np
from jax import lax
from jax.experimental import pallas as pl
from jax.experimental.pallas import tpu as pltpu
from jax.sharding import PartitionSpec as P

HDIM = 128
PW = 32
LEVELS = 3
EPSILON = 1e-06
FLOOR = -1e30
LOG2E = math.log2(math.e)


def frequency_rows():
    half = HDIM // 2
    third = half // 3
    lead = half - 2 * third
    rows = np.zeros((8, HDIM), np.float64)
    for lane in range(HDIM):
        i = lane // 2
        if i < lead:
            rows[0, lane] = 10000.0 ** (-i / lead)
        elif i < lead + third:
            rows[1, lane] = 10000.0 ** (-(i - lead) / third)
        else:
            rows[2, lane] = 10000.0 ** (-(i - lead - third) / third)
    return rows.astype(np.float32)


def rotary_tables(rows, freq):
    frame = lax.axis_index("frames")
    token = lax.axis_index("heads") * rows + lax.broadcasted_iota(jnp.int32, (rows, HDIM), 0)
    even = lax.broadcasted_iota(jnp.int32, (rows, HDIM), 1) % 2 == 0
    angles = (
        frame.astype(jnp.float32) * freq[0:1]
        + (token // PW).astype(jnp.float32) * freq[1:2]
        + (token % PW).astype(jnp.float32) * freq[2:3]
    )
    sine = jnp.sin(angles)
    return jnp.cos(angles), jnp.where(even, -sine, sine), even


def steps_of(count):
    return (0, *range(count - 1, 0, -1))


def block_bases(count, width):
    own_part = lax.axis_index("heads")
    return [pl.multiple_of((own_part ^ step) * width, width) for step in steps_of(count)]


def turn(x_ref, gain_ref, tables, stores, part_width):
    cosine, sine, even = tables
    floats = x_ref[...].astype(jnp.float32)
    inverse = lax.rsqrt(jnp.mean(floats * floats, axis=1, keepdims=True) + EPSILON)
    for base, store in zip(block_bases(len(stores), part_width), stores):
        for offset in range(0, part_width, HDIM):
            at = pl.ds(pl.multiple_of(base + offset, HDIM), HDIM)
            scaled = x_ref[:, at].astype(jnp.float32) * inverse * gain_ref[:, at]
            partner = jnp.where(even, pltpu.roll(scaled, HDIM - 1, 1), pltpu.roll(scaled, 1, 1))
            store(offset, (scaled * cosine + partner * sine).astype(jnp.bfloat16))


def store_in(ref):
    def store(offset, values):
        ref[:, offset : offset + HDIM] = values

    return store


def prepare_kernel(live_hbm, k_hbm, v_hbm, kg_hbm, freq_hbm, q_hbm, qg_hbm, *rest):
    (*block_refs, early_ref, qo_ref, k_ref, kg_ref, freq_ref, q_ref, qg_ref) = rest[:-3]
    live_ref, arrived, placed = rest[-3:]
    rows, width = k_ref.shape
    part_width = width // len(block_refs)
    bases = block_bases(len(block_refs), part_width)
    copies = [
        pltpu.make_async_copy(source, target, arrived.at[number])
        for number, (source, target) in enumerate(
            (
                (freq_hbm, freq_ref),
                (k_hbm, k_ref),
                (kg_hbm, kg_ref),
                (q_hbm, q_ref),
                (qg_hbm, qg_ref),
                (live_hbm, live_ref),
            )
        )
    ]
    copies += [
        pltpu.make_async_copy(
            v_hbm.at[:, pl.ds(base, part_width)],
            block_ref.at[:, part_width:],
            placed.at[step],
        )
        for step, (base, block_ref) in enumerate(zip(bases, block_refs))
    ]
    for copy in copies:
        copy.start()
    copies[0].wait()
    tables = rotary_tables(rows, freq_ref[...])
    copies[1].wait()
    copies[2].wait()
    turn(k_ref, kg_ref, tables, [store_in(ref) for ref in block_refs], part_width)
    for copy in copies[3:]:
        copy.wait()
    live = pick(live_ref, lax.axis_index("frames")) - lax.axis_index("heads") * rows
    for base, block_ref in zip(bases, block_refs):
        two = pooled_floats(pooled(block_ref[...], live, 0), live, 1)
        both = jnp.concatenate([two[:, :part_width], two[:, part_width:]], axis=0)
        early_ref[:, pl.ds(base, part_width)] = both.astype(jnp.bfloat16)
    turn(
        q_ref,
        qg_ref,
        tables,
        [store_in(qo_ref.at[step]) for step in range(len(block_refs))],
        part_width,
    )


def source_of(frame, slot):
    odd = frame % 2
    if slot == "cross":
        return ((frame + 1) ^ 1) - 1
    if slot == "chip":
        return frame ^ 1
    if slot == "ahead":
        return frame + 4 * odd - 2
    if slot == "handed":
        return frame - 4 * odd + 2
    if slot == "four":
        return frame ^ 4
    return ((frame + 4) ^ 4) - 4


def pick(row_ref, index):
    row = row_ref[...]
    lane = lax.broadcasted_iota(jnp.int32, row.shape, 1)
    chosen = jnp.where(lane == index, row, 0).astype(jnp.float32)
    return jnp.sum(chosen, axis=1, keepdims=True).astype(jnp.int32)


def weights_of(live, index, group):
    return jnp.clip(live - index * group, 0, group)


def pooled_floats(values, live, level):
    count = values.shape[0]
    half = count // 2
    group = 2**level
    out_row = lax.broadcasted_iota(jnp.int32, (half, count), 0)
    in_row = lax.broadcasted_iota(jnp.int32, (half, count), 1)
    mix = jnp.where(in_row // 2 == out_row, weights_of(live, in_row, group), 0)
    total = weights_of(live, lax.broadcasted_iota(jnp.int32, (half, 1), 0), 2 * group)
    summed = jnp.dot(
        mix.astype(jnp.float32).astype(jnp.bfloat16), values, preferred_element_type=jnp.float32
    )
    return summed * (1.0 / jnp.maximum(total, 1).astype(jnp.float32))


def pooled(values, live, level):
    return pooled_floats(values, live, level).astype(jnp.bfloat16)


def assemble_kernel(*refs):
    block_refs, own_ref = refs[:-1], refs[-1]
    rows = block_refs[0].shape[0]
    for first, block_ref in zip(block_bases(len(block_refs), rows), block_refs):
        own_ref[pl.ds(first, rows), :] = block_ref[...]


def pool_kernel(live_ref, own_ref, one_ref):
    one_ref[...] = pooled(own_ref[...], pick(live_ref, lax.axis_index("frames")), 0)


def pool_cross_kernel(live_ref, far_ref, out_ref):
    source = source_of(lax.axis_index("frames"), "cross")
    out_ref[...] = pooled(far_ref[...], pick(live_ref, source), 0)


def pack_kernel(four_ref, back_ref, q_ref, *out_refs):
    parts, rows, width = q_ref.shape
    count = four_ref.shape[0]
    for step, (base, out_ref) in enumerate(zip(block_bases(parts, width), out_refs)):
        out_ref[:rows, :] = q_ref[step]
        out_ref[rows : rows + count, :] = four_ref[:, pl.ds(base, width)]
        out_ref[rows + count :, :] = back_ref[:, pl.ds(base, width)]


def selection(in_index, valid, shape, live, level, chosen):
    out_row = lax.broadcasted_iota(jnp.int32, shape, 0)
    group = 2**level
    stay = jnp.where(chosen == level, 1, 0)
    same = jnp.where(in_index == out_row, 1, 0)
    pairs = jnp.where(in_index // 2 == out_row, weights_of(live, in_index, group), 0)
    mix = jnp.where(valid, same * stay + pairs * (1 - stay), 0)
    total = weights_of(live, lax.broadcasted_iota(jnp.int32, (shape[0], 1), 0), 2 * group)
    total = stay + jnp.maximum(total, 1) * (1 - stay)
    return mix.astype(jnp.float32).astype(jnp.bfloat16), total.astype(jnp.float32)


def mixed(mix, values, total):
    summed = jnp.dot(mix, values, preferred_element_type=jnp.float32)
    return (summed * (1.0 / total)).astype(jnp.bfloat16)


SLOTS = ("cross", "chip", "ahead", "handed", "four", "back")


def attend_kernel(keep_ref, level_ref, live_ref, own_ref, *rest):
    (*refs, result_ref, q_ref, kv_ref, bias_ref, early_ref) = rest
    parts = (len(refs) - 4) // 2
    far_refs, packed_refs, out_refs = refs[:4], refs[4 : 4 + parts], refs[4 + parts :]
    tokens, width = q_ref.shape
    rows = tokens // parts
    early_rows = (packed_refs[0].shape[0] - rows) // 2
    groups = early_rows // 2
    frame = lax.axis_index("frames")
    own_live = pick(live_ref, frame)

    def bias_row(live, count, group, active):
        weight = weights_of(live, lax.broadcasted_iota(jnp.int32, (8, count), 1), group)
        logs = jnp.log(jnp.maximum(weight, 1).astype(jnp.float32)) * LOG2E
        return jnp.where(weight * active > 0, logs, FLOOR)

    for first, packed_ref in zip(block_bases(parts, rows), packed_refs):
        q_ref[pl.ds(first, rows), :] = packed_ref[:rows, :]
    kv_ref[0:tokens, :] = own_ref[...]
    bias_ref[:, 0:tokens] = bias_row(own_live, tokens, 1, 1)
    at = tokens
    for number, slot in enumerate(SLOTS):
        level, kind = number // 2, number % 2
        count = tokens >> level
        source = source_of(frame, slot)
        chosen = pick(level_ref, source)
        live = pick(live_ref, source)
        kept = jnp.where(pick(keep_ref, source) == 1, 1, 0)
        low, high = jnp.where(chosen == level, 1, 0), jnp.where(chosen == level + 1, 1, 0)
        active = kept * (low + high)
        group = 2 ** (level + 1) - low * 2**level
        bias_ref[:, at : at + count] = bias_row(live, count, group, active)
        if number < len(far_refs):
            in_index = lax.broadcasted_iota(jnp.int32, (count, count), 1)
            mix, total = selection(in_index, True, (count, count), live, level, chosen)
            kv_ref[at : at + count, :] = mixed(mix, far_refs[number][...], total)
        else:
            skip = rows + kind * early_rows
            for step, packed_ref in enumerate(packed_refs):
                early_ref[kind, step * early_rows : (step + 1) * early_rows, :] = packed_ref[
                    skip : skip + early_rows, :
                ]
            shape = (count, parts * early_rows)
            in_row = lax.broadcasted_iota(jnp.int32, shape, 1)
            inner = in_row % early_rows
            block = in_row // early_rows
            step = jnp.where(block == 0, 0, parts - block)
            part = step ^ lax.axis_index("heads")
            in_index = part * groups + inner % groups
            for half in range(2):
                valid = inner // groups == half
                mix, total = selection(in_index, valid, shape, live, level, chosen)
                kv_ref[at : at + count, half * width : (half + 1) * width] = mixed(
                    mix, early_ref[kind], total
                )
        at += count
    bias = bias_ref[0:1, :]
    alive = lax.broadcasted_iota(jnp.int32, (tokens, 1), 0) < own_live
    for head in range(width // HDIM):
        columns = slice(head * HDIM, (head + 1) * HDIM)
        scores = lax.dot_general(
            q_ref[:, columns],
            kv_ref[:, columns],
            (((1,), (1,)), ((), ())),
            preferred_element_type=jnp.float32,
        )
        scores = scores * (LOG2E / math.sqrt(HDIM)) + bias
        probs = jnp.exp2(scores - jnp.max(scores, axis=1, keepdims=True))
        denominator = jnp.sum(probs, axis=1, keepdims=True)
        numerator = jnp.dot(
            probs.astype(jnp.bfloat16),
            kv_ref[:, width + head * HDIM : width + (head + 1) * HDIM],
            preferred_element_type=jnp.float32,
        )
        result = jnp.where(alive, numerator * (1.0 / denominator), 0.0)
        result_ref[:, columns] = result.astype(jnp.bfloat16)
    for first, out_ref in zip(block_bases(parts, rows), out_refs):
        out_ref[...] = result_ref[pl.ds(first, rows), :]


def place_kernel(*refs):
    block_refs, (out_ref, placed) = refs[:-2], refs[-2:]
    width = block_refs[0].shape[1]
    copies = [
        pltpu.make_async_copy(block_ref, out_ref.at[:, pl.ds(base, width)], placed.at[step])
        for step, (base, block_ref) in enumerate(
            zip(block_bases(len(block_refs), width), block_refs)
        )
    ]
    for copy in copies:
        copy.start()
    for copy in copies:
        copy.wait()


def shards(query_in, key_in, value_in, query_gain, key_gain, keep_flags, pool_levels, live_counts):
    rows, features = query_in.shape
    parts = lax.axis_size("heads")
    frames = lax.axis_size("frames")
    tokens = rows * parts
    width = features // parts
    vmem = pl.BlockSpec(memory_space=pltpu.VMEM)
    live_row = live_counts.reshape(1, frames)
    params = pltpu.CompilerParams(vmem_limit_bytes=32 * 2**20)
    alone = pltpu.CompilerParams(vmem_limit_bytes=60 * 2**20)
    bf16 = jnp.bfloat16

    anywhere = pl.BlockSpec(memory_space=pl.ANY)
    early_rows = 2 * rows >> (LEVELS - 1)
    floats = jnp.float32
    freq = jnp.asarray(frequency_rows())

    def array(*shape):
        return jax.ShapeDtypeStruct(shape, bf16)

    *blocks, early, query_blocks = pl.pallas_call(
        prepare_kernel,
        out_shape=[array(rows, 2 * width)] * parts
        + [array(early_rows, features), array(parts, rows, width)],
        in_specs=[anywhere] * 7,
        out_specs=[vmem] * (parts + 2),
        scratch_shapes=[
            pltpu.VMEM((rows, features), bf16),
            pltpu.VMEM((1, features), floats),
            pltpu.VMEM((8, HDIM), floats),
            pltpu.VMEM((rows, features), bf16),
            pltpu.VMEM((1, features), floats),
            pltpu.VMEM((1, frames), jnp.int32),
            pltpu.SemaphoreType.DMA((6,)),
            pltpu.SemaphoreType.DMA((parts,)),
        ],
        compiler_params=alone,
        name="prepare",
    )(
        live_row,
        key_in,
        value_in,
        key_gain.reshape(1, features),
        freq,
        query_in,
        query_gain.reshape(1, features),
    )

    def permuted(values, slot):
        pairs = []
        for frame in range(frames):
            source = source_of(frame, slot)
            for part in range(parts):
                there = frame * parts + part
                if 0 <= source < frames:
                    pairs.append((source * parts + part, there))
                elif slot == "ahead":
                    pairs.append(((frame ^ 1) * parts + part, there))
                else:
                    pairs.append((frame * parts + (part ^ 1), there))
        return lax.ppermute(values, ("frames", "heads"), pairs)

    def over_parts(blocks):
        return [blocks[0]] + [
            lax.ppermute(block, "heads", [(i, i ^ step) for i in range(parts)])
            for step, block in zip(steps_of(parts)[1:], blocks[1:])
        ]

    blocks = over_parts(blocks)
    four, back = permuted(early, "four"), permuted(early, "back")
    own = pl.pallas_call(
        assemble_kernel,
        out_shape=array(tokens, 2 * width),
        in_specs=[vmem] * parts,
        out_specs=vmem,
        compiler_params=params,
        name="assemble",
    )(*blocks)
    own, four, back = lax.optimization_barrier((own, four, back))
    cross, chip = permuted(own, "cross"), permuted(own, "chip")
    one = pl.pallas_call(
        pool_kernel,
        out_shape=array(tokens // 2, 2 * width),
        in_specs=[vmem, vmem],
        out_specs=vmem,
        compiler_params=params,
        name="pool",
    )(live_row, own)
    ahead = permuted(one, "ahead")
    four, back, chip = lax.optimization_barrier((four, back, chip))
    packed = pl.pallas_call(
        pack_kernel,
        out_shape=[array(rows + 2 * early_rows, width)] * parts,
        in_specs=[vmem] * 3,
        out_specs=[vmem] * parts,
        compiler_params=params,
        name="pack",
    )(four, back, query_blocks)
    packed = over_parts(packed)

    cross, *packed = lax.optimization_barrier((cross, *packed))
    cross_one = pl.pallas_call(
        pool_cross_kernel,
        out_shape=jax.ShapeDtypeStruct((tokens // 2, 2 * width), bf16),
        in_specs=[vmem, vmem],
        out_specs=vmem,
        compiler_params=params,
        name="pool_cross",
    )(live_row, cross)
    far = (cross, chip, ahead, permuted(cross_one, "chip"))
    count = tokens + 2 * sum(tokens >> level for level in range(LEVELS))
    attended = pl.pallas_call(
        attend_kernel,
        out_shape=[array(rows, width)] * parts,
        in_specs=[vmem] * (4 + len(far) + parts),
        out_specs=[vmem] * parts,
        scratch_shapes=[
            pltpu.VMEM((tokens, width), bf16),
            pltpu.VMEM((tokens, width), bf16),
            pltpu.VMEM((count, 2 * width), bf16),
            pltpu.VMEM((8, count), jnp.float32),
            pltpu.VMEM((2, parts * early_rows, width), bf16),
        ],
        compiler_params=params,
        name="attend",
    )(keep_flags, pool_levels, live_row, own, *far, *packed)
    return pl.pallas_call(
        place_kernel,
        out_shape=array(rows, features),
        in_specs=[vmem] * parts,
        out_specs=anywhere,
        scratch_shapes=[pltpu.SemaphoreType.DMA((parts,))],
        compiler_params=params,
        name="place",
    )(*over_parts(attended))


def solution(mesh):
    placed = (
        P(("frames", "heads"), None),
        P(("frames", "heads"), None),
        P(("frames", "heads"), None),
        P(),
        P(),
        P("frames", None),
        P("frames", None),
        P(),
    )
    return jax.shard_map(
        shards, mesh=mesh, in_specs=placed, out_specs=P(("frames", "heads"), None), check_vma=False
    )
```

```python
import math

import jax
import jax.numpy as jnp
import numpy as np
from jax import lax
from jax.experimental import pallas as pl
from jax.experimental.pallas import tpu as pltpu
from jax.sharding import PartitionSpec as P

HDIM = 128
PW = 32
LEVELS = 3
EPSILON = 1e-06
FLOOR = -1e30
LOG2E = math.log2(math.e)


def frequency_rows():
    half = HDIM // 2
    third = half // 3
    lead = half - 2 * third
    rows = np.zeros((8, HDIM), np.float64)
    for lane in range(HDIM):
        i = lane // 2
        if i < lead:
            rows[0, lane] = 10000.0 ** (-i / lead)
        elif i < lead + third:
            rows[1, lane] = 10000.0 ** (-(i - lead) / third)
        else:
            rows[2, lane] = 10000.0 ** (-(i - lead - third) / third)
    return rows.astype(np.float32)


def rotary_tables(rows, freq):
    frame = lax.axis_index("frames")
    token = lax.axis_index("heads") * rows + lax.broadcasted_iota(jnp.int32, (rows, HDIM), 0)
    even = lax.broadcasted_iota(jnp.int32, (rows, HDIM), 1) % 2 == 0
    angles = (
        frame.astype(jnp.float32) * freq[0:1]
        + (token // PW).astype(jnp.float32) * freq[1:2]
        + (token % PW).astype(jnp.float32) * freq[2:3]
    )
    sine = jnp.sin(angles)
    return jnp.cos(angles), jnp.where(even, -sine, sine), even


def steps_of(count):
    return (0, *range(count - 1, 0, -1))


def block_bases(count, width):
    own_part = lax.axis_index("heads")
    return [pl.multiple_of((own_part ^ step) * width, width) for step in steps_of(count)]


def turn(x_ref, gain_ref, tables, stores, part_width):
    cosine, sine, even = tables
    floats = x_ref[...].astype(jnp.float32)
    inverse = lax.rsqrt(jnp.mean(floats * floats, axis=1, keepdims=True) + EPSILON)
    for base, store in zip(block_bases(len(stores), part_width), stores):
        for offset in range(0, part_width, HDIM):
            at = pl.ds(pl.multiple_of(base + offset, HDIM), HDIM)
            scaled = x_ref[:, at].astype(jnp.float32) * inverse * gain_ref[:, at]
            partner = jnp.where(even, pltpu.roll(scaled, HDIM - 1, 1), pltpu.roll(scaled, 1, 1))
            store(offset, (scaled * cosine + partner * sine).astype(jnp.bfloat16))


def store_in(ref):
    def store(offset, values):
        ref[:, offset : offset + HDIM] = values

    return store


def prepare_kernel(live_hbm, k_hbm, v_hbm, kg_hbm, freq_hbm, q_hbm, qg_hbm, *rest):
    (*block_refs, early_ref, qo_ref, k_ref, kg_ref, freq_ref, q_ref, qg_ref) = rest[:-3]
    live_ref, arrived, placed = rest[-3:]
    rows, width = k_ref.shape
    part_width = width // len(block_refs)
    bases = block_bases(len(block_refs), part_width)
    copies = [
        pltpu.make_async_copy(source, target, arrived.at[number])
        for number, (source, target) in enumerate(
            (
                (freq_hbm, freq_ref),
                (k_hbm, k_ref),
                (kg_hbm, kg_ref),
                (q_hbm, q_ref),
                (qg_hbm, qg_ref),
                (live_hbm, live_ref),
            )
        )
    ]
    copies += [
        pltpu.make_async_copy(
            v_hbm.at[:, pl.ds(base, part_width)],
            block_ref.at[:, part_width:],
            placed.at[step],
        )
        for step, (base, block_ref) in enumerate(zip(bases, block_refs))
    ]
    for copy in copies:
        copy.start()
    copies[0].wait()
    tables = rotary_tables(rows, freq_ref[...])
    copies[1].wait()
    copies[2].wait()
    turn(k_ref, kg_ref, tables, [store_in(ref) for ref in block_refs], part_width)
    for copy in copies[3:]:
        copy.wait()
    live = pick(live_ref, lax.axis_index("frames")) - lax.axis_index("heads") * rows
    for base, block_ref in zip(bases, block_refs):
        two = pooled_floats(pooled(block_ref[...], live, 0), live, 1)
        both = jnp.concatenate([two[:, :part_width], two[:, part_width:]], axis=0)
        early_ref[:, pl.ds(base, part_width)] = both.astype(jnp.bfloat16)
    turn(
        q_ref,
        qg_ref,
        tables,
        [store_in(qo_ref.at[step]) for step in range(len(block_refs))],
        part_width,
    )


def source_of(frame, slot):
    odd = frame % 2
    if slot == "cross":
        return ((frame + 1) ^ 1) - 1
    if slot == "chip":
        return frame ^ 1
    if slot == "ahead":
        return frame + 4 * odd - 2
    if slot == "handed":
        return frame - 4 * odd + 2
    if slot == "four":
        return frame ^ 4
    return ((frame + 4) ^ 4) - 4


def pick(row_ref, index):
    row = row_ref[...]
    lane = lax.broadcasted_iota(jnp.int32, row.shape, 1)
    chosen = jnp.where(lane == index, row, 0).astype(jnp.float32)
    return jnp.sum(chosen, axis=1, keepdims=True).astype(jnp.int32)


def weights_of(live, index, group):
    return jnp.clip(live - index * group, 0, group)


def pooled_floats(values, live, level):
    count = values.shape[0]
    half = count // 2
    group = 2**level
    out_row = lax.broadcasted_iota(jnp.int32, (half, count), 0)
    in_row = lax.broadcasted_iota(jnp.int32, (half, count), 1)
    mix = jnp.where(in_row // 2 == out_row, weights_of(live, in_row, group), 0)
    total = weights_of(live, lax.broadcasted_iota(jnp.int32, (half, 1), 0), 2 * group)
    summed = jnp.dot(
        mix.astype(jnp.float32).astype(jnp.bfloat16), values, preferred_element_type=jnp.float32
    )
    return summed * (1.0 / jnp.maximum(total, 1).astype(jnp.float32))


def pooled(values, live, level):
    return pooled_floats(values, live, level).astype(jnp.bfloat16)


def assemble_kernel(*refs):
    block_refs, own_ref = refs[:-1], refs[-1]
    rows = block_refs[0].shape[0]
    for first, block_ref in zip(block_bases(len(block_refs), rows), block_refs):
        own_ref[pl.ds(first, rows), :] = block_ref[...]


def pool_kernel(live_ref, own_ref, one_ref):
    one_ref[...] = pooled(own_ref[...], pick(live_ref, lax.axis_index("frames")), 0)


def pool_cross_kernel(live_ref, far_ref, out_ref):
    source = source_of(lax.axis_index("frames"), "cross")
    out_ref[...] = pooled(far_ref[...], pick(live_ref, source), 0)


def pack_kernel(four_ref, back_ref, q_ref, *out_refs):
    parts, rows, width = q_ref.shape
    count = four_ref.shape[0]
    for step, (base, out_ref) in enumerate(zip(block_bases(parts, width), out_refs)):
        out_ref[:rows, :] = q_ref[step]
        out_ref[rows : rows + count, :] = four_ref[:, pl.ds(base, width)]
        out_ref[rows + count :, :] = back_ref[:, pl.ds(base, width)]


def selection(in_index, valid, shape, live, level, chosen):
    out_row = lax.broadcasted_iota(jnp.int32, shape, 0)
    group = 2**level
    stay = jnp.where(chosen == level, 1, 0)
    same = jnp.where(in_index == out_row, 1, 0)
    pairs = jnp.where(in_index // 2 == out_row, weights_of(live, in_index, group), 0)
    mix = jnp.where(valid, same * stay + pairs * (1 - stay), 0)
    total = weights_of(live, lax.broadcasted_iota(jnp.int32, (shape[0], 1), 0), 2 * group)
    total = stay + jnp.maximum(total, 1) * (1 - stay)
    return mix.astype(jnp.float32).astype(jnp.bfloat16), total.astype(jnp.float32)


def mixed(mix, values, total):
    summed = jnp.dot(mix, values, preferred_element_type=jnp.float32)
    return (summed * (1.0 / total)).astype(jnp.bfloat16)


def near_kernel(
    keep_ref, level_ref, live_ref, cross_ref, chip_ref, cross_out, chip_out, keep_out, level_out
):
    frame = lax.axis_index("frames")
    keep_out[...] = keep_ref[...]
    level_out[...] = level_ref[...]
    for slot, far_ref, out_ref in (
        ("cross", cross_ref, cross_out),
        ("chip", chip_ref, chip_out),
    ):
        source = source_of(frame, slot)
        count = far_ref.shape[0]
        in_index = lax.broadcasted_iota(jnp.int32, (count, count), 1)
        mix, total = selection(
            in_index, True, (count, count), pick(live_ref, source), 0, pick(level_ref, source)
        )
        out_ref[...] = mixed(mix, far_ref[...], total)


SLOTS = ("cross", "chip", "ahead", "handed", "four", "back")


def attend_kernel(keep_ref, level_ref, live_ref, own_ref, *rest):
    (*refs, result_ref, q_ref, kv_ref, bias_ref, early_ref) = rest
    parts = (len(refs) - 4) // 2
    far_refs, packed_refs, out_refs = refs[:4], refs[4 : 4 + parts], refs[4 + parts :]
    tokens, width = q_ref.shape
    rows = tokens // parts
    early_rows = (packed_refs[0].shape[0] - rows) // 2
    groups = early_rows // 2
    frame = lax.axis_index("frames")
    own_live = pick(live_ref, frame)

    def bias_row(live, count, group, active):
        weight = weights_of(live, lax.broadcasted_iota(jnp.int32, (8, count), 1), group)
        logs = jnp.log(jnp.maximum(weight, 1).astype(jnp.float32)) * LOG2E
        return jnp.where(weight * active > 0, logs, FLOOR)

    for first, packed_ref in zip(block_bases(parts, rows), packed_refs):
        q_ref[pl.ds(first, rows), :] = packed_ref[:rows, :]
    kv_ref[0:tokens, :] = own_ref[...]
    bias_ref[:, 0:tokens] = bias_row(own_live, tokens, 1, 1)
    at = tokens
    for number, slot in enumerate(SLOTS):
        level, kind = number // 2, number % 2
        count = tokens >> level
        source = source_of(frame, slot)
        chosen = pick(level_ref, source)
        live = pick(live_ref, source)
        kept = jnp.where(pick(keep_ref, source) == 1, 1, 0)
        low, high = jnp.where(chosen == level, 1, 0), jnp.where(chosen == level + 1, 1, 0)
        active = kept * (low + high)
        group = 2 ** (level + 1) - low * 2**level
        bias_ref[:, at : at + count] = bias_row(live, count, group, active)
        if level == 0:
            kv_ref[at : at + count, :] = far_refs[number][...]
        elif number < len(far_refs):
            in_index = lax.broadcasted_iota(jnp.int32, (count, count), 1)
            mix, total = selection(in_index, True, (count, count), live, level, chosen)
            kv_ref[at : at + count, :] = mixed(mix, far_refs[number][...], total)
        else:
            skip = rows + kind * early_rows
            for step, packed_ref in enumerate(packed_refs):
                early_ref[kind, step * early_rows : (step + 1) * early_rows, :] = packed_ref[
                    skip : skip + early_rows, :
                ]
            shape = (count, parts * early_rows)
            in_row = lax.broadcasted_iota(jnp.int32, shape, 1)
            inner = in_row % early_rows
            block = in_row // early_rows
            step = jnp.where(block == 0, 0, parts - block)
            part = step ^ lax.axis_index("heads")
            in_index = part * groups + inner % groups
            for half in range(2):
                valid = inner // groups == half
                mix, total = selection(in_index, valid, shape, live, level, chosen)
                kv_ref[at : at + count, half * width : (half + 1) * width] = mixed(
                    mix, early_ref[kind], total
                )
        at += count
    bias = bias_ref[0:1, :]
    alive = lax.broadcasted_iota(jnp.int32, (tokens, 1), 0) < own_live
    heads = width // HDIM
    columns = [slice(head * HDIM, (head + 1) * HDIM) for head in range(heads)]

    def scored(head):
        scores = lax.dot_general(
            q_ref[:, columns[head]],
            kv_ref[:, columns[head]],
            (((1,), (1,)), ((), ())),
            preferred_element_type=jnp.float32,
        )
        return scores * (LOG2E / math.sqrt(HDIM)) + bias

    def summed(head, probs, inverse):
        numerator = jnp.dot(
            probs,
            kv_ref[:, width + head * HDIM : width + (head + 1) * HDIM],
            preferred_element_type=jnp.float32,
        )
        result = jnp.where(alive, numerator * inverse, 0.0)
        result_ref[:, columns[head]] = result.astype(jnp.bfloat16)

    scores, waiting = scored(0), None
    for head in range(heads):
        following = scored(head + 1) if head + 1 < heads else None
        if waiting is not None:
            summed(*waiting)
        probs = jnp.exp2(scores - jnp.max(scores, axis=1, keepdims=True))
        inverse = 1.0 / jnp.sum(probs, axis=1, keepdims=True)
        waiting = (head, probs.astype(jnp.bfloat16), inverse)
        scores = following
    summed(*waiting)
    for first, out_ref in zip(block_bases(parts, rows), out_refs):
        out_ref[...] = result_ref[pl.ds(first, rows), :]


def place_kernel(*refs):
    block_refs, (out_ref, placed) = refs[:-2], refs[-2:]
    width = block_refs[0].shape[1]
    copies = [
        pltpu.make_async_copy(block_ref, out_ref.at[:, pl.ds(base, width)], placed.at[step])
        for step, (base, block_ref) in enumerate(
            zip(block_bases(len(block_refs), width), block_refs)
        )
    ]
    for copy in copies:
        copy.start()
    for copy in copies:
        copy.wait()


def shards(query_in, key_in, value_in, query_gain, key_gain, keep_flags, pool_levels, live_counts):
    rows, features = query_in.shape
    parts = lax.axis_size("heads")
    frames = lax.axis_size("frames")
    tokens = rows * parts
    width = features // parts
    vmem = pl.BlockSpec(memory_space=pltpu.VMEM)
    live_row = live_counts.reshape(1, frames)
    params = pltpu.CompilerParams(vmem_limit_bytes=32 * 2**20)
    alone = pltpu.CompilerParams(vmem_limit_bytes=60 * 2**20)
    bf16 = jnp.bfloat16

    anywhere = pl.BlockSpec(memory_space=pl.ANY)
    early_rows = 2 * rows >> (LEVELS - 1)
    floats = jnp.float32
    freq = jnp.asarray(frequency_rows())

    def array(*shape):
        return jax.ShapeDtypeStruct(shape, bf16)

    *blocks, early, query_blocks = pl.pallas_call(
        prepare_kernel,
        out_shape=[array(rows, 2 * width)] * parts
        + [array(early_rows, features), array(parts, rows, width)],
        in_specs=[anywhere] * 7,
        out_specs=[vmem] * (parts + 2),
        scratch_shapes=[
            pltpu.VMEM((rows, features), bf16),
            pltpu.VMEM((1, features), floats),
            pltpu.VMEM((8, HDIM), floats),
            pltpu.VMEM((rows, features), bf16),
            pltpu.VMEM((1, features), floats),
            pltpu.VMEM((1, frames), jnp.int32),
            pltpu.SemaphoreType.DMA((6,)),
            pltpu.SemaphoreType.DMA((parts,)),
        ],
        compiler_params=alone,
        name="prepare",
    )(
        live_row,
        key_in,
        value_in,
        key_gain.reshape(1, features),
        freq,
        query_in,
        query_gain.reshape(1, features),
    )

    def permuted(values, slot):
        pairs = []
        for frame in range(frames):
            source = source_of(frame, slot)
            for part in range(parts):
                there = frame * parts + part
                if 0 <= source < frames:
                    pairs.append((source * parts + part, there))
                elif slot == "ahead":
                    pairs.append(((frame ^ 1) * parts + part, there))
                else:
                    pairs.append((frame * parts + (part ^ 1), there))
        return lax.ppermute(values, ("frames", "heads"), pairs)

    def over_parts(blocks):
        return [blocks[0]] + [
            lax.ppermute(block, "heads", [(i, i ^ step) for i in range(parts)])
            for step, block in zip(steps_of(parts)[1:], blocks[1:])
        ]

    blocks = over_parts(blocks)
    four, back = permuted(early, "four"), permuted(early, "back")
    own = pl.pallas_call(
        assemble_kernel,
        out_shape=array(tokens, 2 * width),
        in_specs=[vmem] * parts,
        out_specs=vmem,
        compiler_params=params,
        name="assemble",
    )(*blocks)
    own, four, back = lax.optimization_barrier((own, four, back))
    cross, chip = permuted(own, "cross"), permuted(own, "chip")
    one = pl.pallas_call(
        pool_kernel,
        out_shape=array(tokens // 2, 2 * width),
        in_specs=[vmem, vmem],
        out_specs=vmem,
        compiler_params=params,
        name="pool",
    )(live_row, own)
    ahead = permuted(one, "ahead")
    four, back, chip = lax.optimization_barrier((four, back, chip))
    packed = pl.pallas_call(
        pack_kernel,
        out_shape=[array(rows + 2 * early_rows, width)] * parts,
        in_specs=[vmem] * 3,
        out_specs=[vmem] * parts,
        compiler_params=params,
        name="pack",
    )(four, back, query_blocks)
    packed = over_parts(packed)

    cross, *packed = lax.optimization_barrier((cross, *packed))
    cross_one = pl.pallas_call(
        pool_cross_kernel,
        out_shape=jax.ShapeDtypeStruct((tokens // 2, 2 * width), bf16),
        in_specs=[vmem, vmem],
        out_specs=vmem,
        compiler_params=params,
        name="pool_cross",
    )(live_row, cross)
    handed = permuted(cross_one, "chip")
    cross, chip, keep_row, level_row = pl.pallas_call(
        near_kernel,
        out_shape=[array(tokens, 2 * width)] * 2
        + [jax.ShapeDtypeStruct((1, frames), jnp.int32)] * 2,
        in_specs=[vmem] * 5,
        out_specs=[vmem] * 4,
        compiler_params=params,
        name="near",
    )(keep_flags, pool_levels, live_row, cross, chip)
    far = (cross, chip, ahead, handed)
    count = tokens + 2 * sum(tokens >> level for level in range(LEVELS))
    attended = pl.pallas_call(
        attend_kernel,
        out_shape=[array(rows, width)] * parts,
        in_specs=[vmem] * (4 + len(far) + parts),
        out_specs=[vmem] * parts,
        scratch_shapes=[
            pltpu.VMEM((tokens, width), bf16),
            pltpu.VMEM((tokens, width), bf16),
            pltpu.VMEM((count, 2 * width), bf16),
            pltpu.VMEM((8, count), jnp.float32),
            pltpu.VMEM((2, parts * early_rows, width), bf16),
        ],
        compiler_params=params,
        name="attend",
    )(keep_row, level_row, live_row, own, *far, *packed)
    return pl.pallas_call(
        place_kernel,
        out_shape=array(rows, features),
        in_specs=[vmem] * parts,
        out_specs=anywhere,
        scratch_shapes=[pltpu.SemaphoreType.DMA((parts,))],
        compiler_params=params,
        name="place",
    )(*over_parts(attended))


def solution(mesh):
    placed = (
        P(("frames", "heads"), None),
        P(("frames", "heads"), None),
        P(("frames", "heads"), None),
        P(),
        P(),
        P("frames", None),
        P("frames", None),
        P(),
    )
    return jax.shard_map(
        shards, mesh=mesh, in_specs=placed, out_specs=P(("frames", "heads"), None), check_vma=False
    )
```

```python
import math

import jax
import jax.numpy as jnp
import numpy as np
from jax import lax
from jax.experimental import pallas as pl
from jax.experimental.pallas import tpu as pltpu
from jax.sharding import PartitionSpec as P

HDIM = 128
PW = 32
LEVELS = 3
EPSILON = 1e-06
FLOOR = -1e30
LOG2E = math.log2(math.e)


def frequency_rows():
    half = HDIM // 2
    third = half // 3
    lead = half - 2 * third
    rows = np.zeros((8, HDIM), np.float64)
    for lane in range(HDIM):
        i = lane // 2
        if i < lead:
            rows[0, lane] = 10000.0 ** (-i / lead)
        elif i < lead + third:
            rows[1, lane] = 10000.0 ** (-(i - lead) / third)
        else:
            rows[2, lane] = 10000.0 ** (-(i - lead - third) / third)
    return rows.astype(np.float32)


def rotary_tables(rows, freq):
    frame = lax.axis_index("frames")
    token = lax.axis_index("heads") * rows + lax.broadcasted_iota(jnp.int32, (rows, HDIM), 0)
    even = lax.broadcasted_iota(jnp.int32, (rows, HDIM), 1) % 2 == 0
    angles = (
        frame.astype(jnp.float32) * freq[0:1]
        + (token // PW).astype(jnp.float32) * freq[1:2]
        + (token % PW).astype(jnp.float32) * freq[2:3]
    )
    sine = jnp.sin(angles)
    return jnp.cos(angles), jnp.where(even, -sine, sine), even


def steps_of(count):
    return (0, *range(count - 1, 0, -1))


def block_bases(count, width):
    own_part = lax.axis_index("heads")
    return [pl.multiple_of((own_part ^ step) * width, width) for step in steps_of(count)]


def turn(x_ref, gain_ref, tables, stores, part_width):
    cosine, sine, even = tables
    floats = x_ref[...].astype(jnp.float32)
    inverse = lax.rsqrt(jnp.mean(floats * floats, axis=1, keepdims=True) + EPSILON)
    for base, store in zip(block_bases(len(stores), part_width), stores):
        for offset in range(0, part_width, HDIM):
            at = pl.ds(pl.multiple_of(base + offset, HDIM), HDIM)
            scaled = x_ref[:, at].astype(jnp.float32) * inverse * gain_ref[:, at]
            partner = jnp.where(even, pltpu.roll(scaled, HDIM - 1, 1), pltpu.roll(scaled, 1, 1))
            store(offset, (scaled * cosine + partner * sine).astype(jnp.bfloat16))


def store_in(ref):
    def store(offset, values):
        ref[:, offset : offset + HDIM] = values

    return store


def prepare_kernel(live_hbm, k_hbm, v_hbm, kg_hbm, freq_hbm, q_hbm, qg_hbm, *rest):
    (*block_refs, early_ref, qo_ref, k_ref, kg_ref, freq_ref, q_ref, qg_ref) = rest[:-3]
    live_ref, arrived, placed = rest[-3:]
    rows, width = k_ref.shape
    part_width = width // len(block_refs)
    bases = block_bases(len(block_refs), part_width)
    copies = [
        pltpu.make_async_copy(source, target, arrived.at[number])
        for number, (source, target) in enumerate(
            (
                (freq_hbm, freq_ref),
                (k_hbm, k_ref),
                (kg_hbm, kg_ref),
                (q_hbm, q_ref),
                (qg_hbm, qg_ref),
                (live_hbm, live_ref),
            )
        )
    ]
    copies += [
        pltpu.make_async_copy(
            v_hbm.at[:, pl.ds(base, part_width)],
            block_ref.at[:, part_width:],
            placed.at[step],
        )
        for step, (base, block_ref) in enumerate(zip(bases, block_refs))
    ]
    for copy in copies:
        copy.start()
    copies[0].wait()
    tables = rotary_tables(rows, freq_ref[...])
    copies[1].wait()
    copies[2].wait()
    turn(k_ref, kg_ref, tables, [store_in(ref) for ref in block_refs], part_width)
    for copy in copies[3:]:
        copy.wait()
    live = pick(live_ref, lax.axis_index("frames")) - lax.axis_index("heads") * rows
    for base, block_ref in zip(bases, block_refs):
        two = pooled_floats(pooled(block_ref[...], live, 0), live, 1)
        both = jnp.concatenate([two[:, :part_width], two[:, part_width:]], axis=0)
        early_ref[:, pl.ds(base, part_width)] = both.astype(jnp.bfloat16)
    turn(
        q_ref,
        qg_ref,
        tables,
        [store_in(qo_ref.at[step]) for step in range(len(block_refs))],
        part_width,
    )


def source_of(frame, slot):
    odd = frame % 2
    if slot == "cross":
        return ((frame + 1) ^ 1) - 1
    if slot == "chip":
        return frame ^ 1
    if slot == "ahead":
        return frame + 4 * odd - 2
    if slot == "handed":
        return frame - 4 * odd + 2
    if slot == "four":
        return frame ^ 4
    return ((frame + 4) ^ 4) - 4


def pick(row_ref, index):
    row = row_ref[...]
    lane = lax.broadcasted_iota(jnp.int32, row.shape, 1)
    chosen = jnp.where(lane == index, row, 0).astype(jnp.float32)
    return jnp.sum(chosen, axis=1, keepdims=True).astype(jnp.int32)


def weights_of(live, index, group):
    return jnp.clip(live - index * group, 0, group)


def pooled_floats(values, live, level):
    count = values.shape[0]
    half = count // 2
    group = 2**level
    out_row = lax.broadcasted_iota(jnp.int32, (half, count), 0)
    in_row = lax.broadcasted_iota(jnp.int32, (half, count), 1)
    mix = jnp.where(in_row // 2 == out_row, weights_of(live, in_row, group), 0)
    total = weights_of(live, lax.broadcasted_iota(jnp.int32, (half, 1), 0), 2 * group)
    summed = jnp.dot(
        mix.astype(jnp.float32).astype(jnp.bfloat16), values, preferred_element_type=jnp.float32
    )
    return summed * (1.0 / jnp.maximum(total, 1).astype(jnp.float32))


def pooled(values, live, level):
    return pooled_floats(values, live, level).astype(jnp.bfloat16)


def assemble_kernel(*refs):
    block_refs, own_ref = refs[:-1], refs[-1]
    rows = block_refs[0].shape[0]
    for first, block_ref in zip(block_bases(len(block_refs), rows), block_refs):
        own_ref[pl.ds(first, rows), :] = block_ref[...]


def pool_kernel(live_ref, own_ref, one_ref):
    one_ref[...] = pooled(own_ref[...], pick(live_ref, lax.axis_index("frames")), 0)


def pool_cross_kernel(live_ref, far_ref, out_ref):
    source = source_of(lax.axis_index("frames"), "cross")
    out_ref[...] = pooled(far_ref[...], pick(live_ref, source), 0)


def pack_kernel(four_ref, back_ref, q_ref, *out_refs):
    parts, rows, width = q_ref.shape
    count = four_ref.shape[0]
    for step, (base, out_ref) in enumerate(zip(block_bases(parts, width), out_refs)):
        out_ref[:rows, :] = q_ref[step]
        out_ref[rows : rows + count, :] = four_ref[:, pl.ds(base, width)]
        out_ref[rows + count :, :] = back_ref[:, pl.ds(base, width)]


def selection(in_index, valid, shape, live, level, chosen):
    out_row = lax.broadcasted_iota(jnp.int32, shape, 0)
    group = 2**level
    stay = jnp.where(chosen == level, 1, 0)
    same = jnp.where(in_index == out_row, 1, 0)
    pairs = jnp.where(in_index // 2 == out_row, weights_of(live, in_index, group), 0)
    mix = jnp.where(valid, same * stay + pairs * (1 - stay), 0)
    total = weights_of(live, lax.broadcasted_iota(jnp.int32, (shape[0], 1), 0), 2 * group)
    total = stay + jnp.maximum(total, 1) * (1 - stay)
    return mix.astype(jnp.float32).astype(jnp.bfloat16), total.astype(jnp.float32)


def mixed(mix, values, total):
    summed = jnp.dot(mix, values, preferred_element_type=jnp.float32)
    return (summed * (1.0 / total)).astype(jnp.bfloat16)


def near_kernel(
    keep_ref, level_ref, live_ref, cross_ref, chip_ref, cross_out, chip_out, keep_out, level_out
):
    frame = lax.axis_index("frames")
    keep_out[...] = keep_ref[...]
    level_out[...] = level_ref[...]
    for slot, far_ref, out_ref in (
        ("cross", cross_ref, cross_out),
        ("chip", chip_ref, chip_out),
    ):
        source = source_of(frame, slot)
        count = far_ref.shape[0]
        in_index = lax.broadcasted_iota(jnp.int32, (count, count), 1)
        mix, total = selection(
            in_index, True, (count, count), pick(live_ref, source), 0, pick(level_ref, source)
        )
        out_ref[...] = mixed(mix, far_ref[...], total)


SLOTS = ("cross", "chip", "ahead", "handed", "four", "back")


def attend_kernel(keep_ref, level_ref, live_ref, own_ref, *rest):
    (*refs, result_ref, q_ref, kv_ref, bias_ref, early_ref) = rest
    parts = (len(refs) - 4) // 2
    far_refs, packed_refs, out_refs = refs[:4], refs[4 : 4 + parts], refs[4 + parts :]
    tokens, width = q_ref.shape
    rows = tokens // parts
    early_rows = (packed_refs[0].shape[0] - rows) // 2
    groups = early_rows // 2
    frame = lax.axis_index("frames")
    own_live = pick(live_ref, frame)

    def bias_row(live, count, group, active):
        weight = weights_of(live, lax.broadcasted_iota(jnp.int32, (8, count), 1), group)
        logs = jnp.log(jnp.maximum(weight, 1).astype(jnp.float32)) * LOG2E
        return jnp.where(weight * active > 0, logs, FLOOR)

    for first, packed_ref in zip(block_bases(parts, rows), packed_refs):
        q_ref[pl.ds(first, rows), :] = packed_ref[:rows, :]
    kv_ref[0:tokens, :] = own_ref[...]
    bias_ref[:, 0:tokens] = bias_row(own_live, tokens, 1, 1)
    at = tokens
    for number, slot in enumerate(SLOTS):
        level, kind = number // 2, number % 2
        count = tokens >> level
        source = source_of(frame, slot)
        chosen = pick(level_ref, source)
        live = pick(live_ref, source)
        kept = jnp.where(pick(keep_ref, source) == 1, 1, 0)
        low, high = jnp.where(chosen == level, 1, 0), jnp.where(chosen == level + 1, 1, 0)
        active = kept * (low + high)
        group = 2 ** (level + 1) - low * 2**level
        bias_ref[:, at : at + count] = bias_row(live, count, group, active)
        if level == 0:
            kv_ref[at : at + count, :] = far_refs[number][...]
        elif number < len(far_refs):
            in_index = lax.broadcasted_iota(jnp.int32, (count, count), 1)
            mix, total = selection(in_index, True, (count, count), live, level, chosen)
            kv_ref[at : at + count, :] = mixed(mix, far_refs[number][...], total)
        else:
            skip = rows + kind * early_rows
            for step, packed_ref in enumerate(packed_refs):
                early_ref[kind, step * early_rows : (step + 1) * early_rows, :] = packed_ref[
                    skip : skip + early_rows, :
                ]
            shape = (count, parts * early_rows)
            in_row = lax.broadcasted_iota(jnp.int32, shape, 1)
            inner = in_row % early_rows
            block = in_row // early_rows
            step = jnp.where(block == 0, 0, parts - block)
            part = step ^ lax.axis_index("heads")
            in_index = part * groups + inner % groups
            for half in range(2):
                valid = inner // groups == half
                mix, total = selection(in_index, valid, shape, live, level, chosen)
                kv_ref[at : at + count, half * width : (half + 1) * width] = mixed(
                    mix, early_ref[kind], total
                )
        at += count
    bias = bias_ref[0:1, :]
    alive = lax.broadcasted_iota(jnp.int32, (tokens, 1), 0) < own_live
    heads = width // HDIM
    columns = [slice(head * HDIM, (head + 1) * HDIM) for head in range(heads)]

    def scored(head):
        scores = lax.dot_general(
            q_ref[:, columns[head]],
            kv_ref[:, columns[head]],
            (((1,), (1,)), ((), ())),
            preferred_element_type=jnp.float32,
        )
        return scores * (LOG2E / math.sqrt(HDIM)) + bias

    def summed(head, probs, inverse):
        numerator = jnp.dot(
            probs,
            kv_ref[:, width + head * HDIM : width + (head + 1) * HDIM],
            preferred_element_type=jnp.float32,
        )
        result = jnp.where(alive, numerator * inverse, 0.0)
        result_ref[:, columns[head]] = result.astype(jnp.bfloat16)

    scores, waiting = scored(0), None
    for head in range(heads):
        following = scored(head + 1) if head + 1 < heads else None
        if waiting is not None:
            summed(*waiting)
        probs = jnp.exp2(scores - jnp.max(scores, axis=1, keepdims=True))
        inverse = 1.0 / jnp.sum(probs, axis=1, keepdims=True)
        waiting = (head, probs.astype(jnp.bfloat16), inverse)
        scores = following
    summed(*waiting)
    for first, out_ref in zip(block_bases(parts, rows), out_refs):
        out_ref[...] = result_ref[pl.ds(first, rows), :]


def place_kernel(*refs):
    block_refs, (out_ref, placed) = refs[:-2], refs[-2:]
    width = block_refs[0].shape[1]
    copies = [
        pltpu.make_async_copy(block_ref, out_ref.at[:, pl.ds(base, width)], placed.at[step])
        for step, (base, block_ref) in enumerate(
            zip(block_bases(len(block_refs), width), block_refs)
        )
    ]
    for copy in copies:
        copy.start()
    for copy in copies:
        copy.wait()


def shards(query_in, key_in, value_in, query_gain, key_gain, keep_flags, pool_levels, live_counts):
    rows, features = query_in.shape
    parts = lax.axis_size("heads")
    frames = lax.axis_size("frames")
    tokens = rows * parts
    width = features // parts
    vmem = pl.BlockSpec(memory_space=pltpu.VMEM)
    live_row = live_counts.reshape(1, frames)
    params = pltpu.CompilerParams(vmem_limit_bytes=32 * 2**20)
    alone = pltpu.CompilerParams(vmem_limit_bytes=60 * 2**20)
    bf16 = jnp.bfloat16

    anywhere = pl.BlockSpec(memory_space=pl.ANY)
    early_rows = 2 * rows >> (LEVELS - 1)
    floats = jnp.float32
    freq = jnp.asarray(frequency_rows())

    def array(*shape):
        return jax.ShapeDtypeStruct(shape, bf16)

    *blocks, early, query_blocks = pl.pallas_call(
        prepare_kernel,
        out_shape=[array(rows, 2 * width)] * parts
        + [array(early_rows, features), array(parts, rows, width)],
        in_specs=[anywhere] * 7,
        out_specs=[vmem] * (parts + 2),
        scratch_shapes=[
            pltpu.VMEM((rows, features), bf16),
            pltpu.VMEM((1, features), floats),
            pltpu.VMEM((8, HDIM), floats),
            pltpu.VMEM((rows, features), bf16),
            pltpu.VMEM((1, features), floats),
            pltpu.VMEM((1, frames), jnp.int32),
            pltpu.SemaphoreType.DMA((6,)),
            pltpu.SemaphoreType.DMA((parts,)),
        ],
        compiler_params=alone,
        name="prepare",
    )(
        live_row,
        key_in,
        value_in,
        key_gain.reshape(1, features),
        freq,
        query_in,
        query_gain.reshape(1, features),
    )

    def permuted(values, slot):
        pairs = []
        for frame in range(frames):
            source = source_of(frame, slot)
            for part in range(parts):
                there = frame * parts + part
                if 0 <= source < frames:
                    pairs.append((source * parts + part, there))
                elif slot == "ahead":
                    pairs.append(((frame ^ 1) * parts + part, there))
                else:
                    pairs.append((frame * parts + (part ^ 1), there))
        return lax.ppermute(values, ("frames", "heads"), pairs)

    def over_parts(blocks):
        return [blocks[0]] + [
            lax.ppermute(block, "heads", [(i, i ^ step) for i in range(parts)])
            for step, block in zip(steps_of(parts)[1:], blocks[1:])
        ]

    blocks = over_parts(blocks)
    four, back = permuted(early, "four"), permuted(early, "back")
    own = pl.pallas_call(
        assemble_kernel,
        out_shape=array(tokens, 2 * width),
        in_specs=[vmem] * parts,
        out_specs=vmem,
        compiler_params=params,
        name="assemble",
    )(*blocks)
    own, four, back = lax.optimization_barrier((own, four, back))
    cross, chip = permuted(own, "cross"), permuted(own, "chip")
    one = pl.pallas_call(
        pool_kernel,
        out_shape=array(tokens // 2, 2 * width),
        in_specs=[vmem, vmem],
        out_specs=vmem,
        compiler_params=params,
        name="pool",
    )(live_row, own)
    ahead = permuted(one, "ahead")
    chip, back, four = lax.optimization_barrier((chip, back, four))
    packed = pl.pallas_call(
        pack_kernel,
        out_shape=[array(rows + 2 * early_rows, width)] * parts,
        in_specs=[vmem] * 3,
        out_specs=[vmem] * parts,
        compiler_params=params,
        name="pack",
    )(four, back, query_blocks)
    packed = over_parts(packed)

    cross, *packed = lax.optimization_barrier((cross, *packed))
    cross_one = pl.pallas_call(
        pool_cross_kernel,
        out_shape=jax.ShapeDtypeStruct((tokens // 2, 2 * width), bf16),
        in_specs=[vmem, vmem],
        out_specs=vmem,
        compiler_params=params,
        name="pool_cross",
    )(live_row, cross)
    handed = permuted(cross_one, "chip")
    cross, chip, keep_row, level_row = pl.pallas_call(
        near_kernel,
        out_shape=[array(tokens, 2 * width)] * 2
        + [jax.ShapeDtypeStruct((1, frames), jnp.int32)] * 2,
        in_specs=[vmem] * 5,
        out_specs=[vmem] * 4,
        compiler_params=params,
        name="near",
    )(keep_flags, pool_levels, live_row, cross, chip)
    far = (cross, chip, ahead, handed)
    count = tokens + 2 * sum(tokens >> level for level in range(LEVELS))
    attended = pl.pallas_call(
        attend_kernel,
        out_shape=[array(rows, width)] * parts,
        in_specs=[vmem] * (4 + len(far) + parts),
        out_specs=[vmem] * parts,
        scratch_shapes=[
            pltpu.VMEM((tokens, width), bf16),
            pltpu.VMEM((tokens, width), bf16),
            pltpu.VMEM((count, 2 * width), bf16),
            pltpu.VMEM((8, count), jnp.float32),
            pltpu.VMEM((2, parts * early_rows, width), bf16),
        ],
        compiler_params=params,
        name="attend",
    )(keep_row, level_row, live_row, own, *far, *packed)
    return pl.pallas_call(
        place_kernel,
        out_shape=array(rows, features),
        in_specs=[vmem] * parts,
        out_specs=anywhere,
        scratch_shapes=[pltpu.SemaphoreType.DMA((parts,))],
        compiler_params=params,
        name="place",
    )(*over_parts(attended))


def solution(mesh):
    placed = (
        P(("frames", "heads"), None),
        P(("frames", "heads"), None),
        P(("frames", "heads"), None),
        P(),
        P(),
        P("frames", None),
        P("frames", None),
        P(),
    )
    return jax.shard_map(
        shards, mesh=mesh, in_specs=placed, out_specs=P(("frames", "heads"), None), check_vma=False
    )
```
